32 devices in a mesh: pack: 2 (over x), seq: 16 (over z, y, core).
Axes of the slice: x: 2, y: 2, z: 4, core: 2. Of those that a mesh axis runs over, the one named last changes fastest.
Arguments:
- queries: bfloat16 [4096, 2048], P(('pack', 'seq')), parts along dimension 0, may hold values from -48 to 48
- token_key_heads: bfloat16 [4096, 256], P(('pack', 'seq')), parts along dimension 0, may hold values from -6 to 6
- token_value_heads: bfloat16 [4096, 256], P(('pack', 'seq')), parts along dimension 0, may hold values from -6 to 6
- residual: bfloat16 [4096, 1024], P(('pack', 'seq')), parts along dimension 0, may hold values from -40 to 40
- out_weight: bfloat16 [2048, 1024], P('seq'), may hold values from -0.125 to 0.125
- norm_gain: bfloat16 [1024], replicated, may hold values from 0.5 to 1.5
- w_gate: bfloat16 [16, 1024, 384], P('seq'), may hold values from -0.1875 to 0.1875
- w_up: bfloat16 [16, 1024, 384], P('seq'), may hold values from -0.1875 to 0.1875
- w_down: bfloat16 [16, 384, 1024], P('seq'), may hold values from -0.3125 to 0.3125
- expert_ids: int32 [4096, 8], P(('pack', 'seq')), parts along dimension 0, may hold values from 0 to 15, all different within a row; in each aligned block of 128 rows (0 to 127, 128 to 255, ...) at most 96 rows name the same one
- gate_weights: float32 [4096, 8], P(('pack', 'seq')), parts along dimension 0, may hold values from 0.05 to 0.3
- doc_of_block: int32 [32], P('pack'), parts along dimension 0, may hold values from 0 to 3, never falling along the last dimension, each value on 1 to 8 neighbouring positions
Outputs:
- attention: bfloat16 [4096, 2048], P(('pack', 'seq')), parts along dimension 0
- hidden_out: bfloat16 [4096, 1024], P(('pack', 'seq')), parts along dimension 0
- expert_mix: bfloat16 [4096, 1024], P(('pack', 'seq')), parts along dimension 0
The draws below stay inside these ranges and needn't reach their ends.
There are 2 independent parts, one for each index of `pack`. The reference program is written for one: setup_inputs(seed, part) draws one part's arguments, and reference() takes and returns one part's arrays. A program takes and returns all parts, laid end to end along the dimension named above; an argument that names none is the same for every part. Nothing has to cross between parts.
Inputs may be any that keep to these rules, and one draw needn't show every extreme that they name: `expert_ids`: each row names 8 different experts; within the rows of one block no expert is named more than 96 times, and in every draw some expert is named exactly 96 times by the rows of some block. `doc_of_block`: never falls from block to block; each document covers 1 to 8 blocks, one exactly 8.
All inputs are finite; a program needn't handle non-finite values.
Results may differ from the reference program's by a relative error of at most 0.015.
Values may be sent and summed in bfloat16 or wider, within the bound.
No kernel may reach another device: no remote copies, remote signals or barrier semaphores. Data moves between devices by JAX's collectives and lax.ppermute only.
A program may use at most 64 MiB of HBM per device.

```python
import math
import jax
import jax.numpy as jnp
import numpy as np
from jax import lax

D = 1024
FF = 384
QUERY_HEADS = 16
KEY_VALUE_HEADS = 2
HEAD_SIZE = 128
TOP = 8
TOK_DEV = 128
SLAB_TOKENS = 2048
EXPERTS = 16
SLOT = 96
MOST_BLK = 8
DOCS = 4
N_SEQ = 16


def query_key_pair(key):
    base_key = jax.random.fold_in(key, 7103)
    query_key, head_random_key = jax.random.split(base_key, 2)
    query_random_draw = jnp.clip(jax.random.normal(query_key, (SLAB_TOKENS, QUERY_HEADS, HEAD_SIZE), jnp.float32), -6.0, 6.0)
    key_random_draw = jnp.clip(jax.random.normal(head_random_key, (SLAB_TOKENS, KEY_VALUE_HEADS, HEAD_SIZE), jnp.float32), -6.0, 6.0)
    return (query_random_draw.reshape(SLAB_TOKENS, QUERY_HEADS * HEAD_SIZE), key_random_draw.reshape(SLAB_TOKENS, KEY_VALUE_HEADS * HEAD_SIZE))


def draw_queries(key, part):
    return query_key_pair(key)[0].astype(jnp.bfloat16)


def draw_token_key_heads(key, part):
    return query_key_pair(key)[1].astype(jnp.bfloat16)


def draw_residual(key, part):
    base_key = jax.random.fold_in(key, 5081)
    row_key, col_key, jitter_key = jax.random.split(base_key, 3)
    row_scale = jnp.exp(jax.random.uniform(row_key, (SLAB_TOKENS, 1), jnp.float32, math.log(0.3), math.log(3.0)))
    col_scale = jnp.exp(jax.random.uniform(col_key, (1, D), jnp.float32, math.log(0.3), math.log(3.0)))
    jitter = jnp.clip(jax.random.normal(jitter_key, (SLAB_TOKENS, D), jnp.float32), -4.0, 4.0)
    return (jitter * row_scale * col_scale).astype(jnp.bfloat16)


def steps_of(rng, shape, cuts, smallest, top_value):
    gain = 1.0
    for axis_at, shards_of in cuts:
        draws = jax.random.uniform(jax.random.fold_in(jax.random.fold_in(rng, 6), axis_at), (shards_of,), jnp.float32, smallest / len(cuts), top_value / len(cuts))
        gain = gain * jnp.repeat(jnp.exp(draws), shape[axis_at] // shards_of).reshape((-1,) + (1,) * (len(shape) - 1 - axis_at))
    return gain


def length_profile(count, total, reach, skew):
    weights = [(1 << 20) // math.isqrt(rank ** skew) + 1 for rank in range(2, count + 1)]
    spare, holding = total - reach - (count - 1), [1] * (count - 1)
    while spare > 0:
        free = [i for i in range(count - 1) if holding[i] < reach]
        whole, budget = sum([weights[i] for i in free]), spare
        for i in free:
            extra = min(reach - holding[i], max(1, budget * weights[i] // whole), spare)
            holding[i] = holding[i] + extra
            spare = spare - extra
    return np.array([reach] + holding)


def uneven(key, count, total, most, skew):
    if count == 2:
        one = jax.random.randint(key, (), max(1, total - most), min(most, total - 1) + 1)
        return jnp.stack([one, total - one])
    lengths = jnp.asarray(length_profile(count, total, most, skew), jnp.int32)
    couples = (count - 1) // 2
    source_of, receiver = lengths[1:1 + 2 * couples:2], lengths[2:2 + 2 * couples:2]
    margin = jnp.minimum(source_of - 1, most - receiver)
    moved = jax.random.randint(jax.random.fold_in(key, 1), (couples,), 0, 1 << 20) % (margin + 1)
    lengths = lengths.at[1:1 + 2 * couples:2].set(source_of - moved).at[2:2 + 2 * couples:2].set(receiver + moved)
    return lengths[jax.random.permutation(jax.random.fold_in(key, 2), count)]


def assign_block(key, own, number, rows, amount, top, reach, skew):
    ranking = jax.random.permutation(key, amount)
    packed, ordinary = shares(amount, rows * top, reach, skew, True), shares(amount, rows * top, reach, skew, False)
    places = jnp.arange(amount)

    def named(sizes, offset_by):
        used = int((sizes > 0).sum())
        fixed = max(1, used // 4)
        moved = fixed + (places - fixed + offset_by * (used - fixed)) % max(1, amount - fixed)
        return jnp.zeros((amount,), jnp.int32).at[ranking[jnp.where(places < fixed, places, moved)]].set(jnp.asarray(sizes, jnp.int32))

    sizes = jnp.where(number % 4 == 0, named(packed, number // 4), named(ordinary, number - number // 4 - 1))
    mixed = jax.random.permutation(jax.random.fold_in(own, 3), amount)
    donor, receiver = mixed[0:amount // 2 * 2:2], mixed[1:amount // 2 * 2:2]
    margin = jnp.minimum(sizes[donor] - 1, reach - sizes[receiver]) // 2
    margin = jnp.where((donor == ranking[0]) | (receiver == ranking[0]) | (sizes[receiver] == 0), 0, jnp.maximum(margin, 0))
    moved = jax.random.randint(jax.random.fold_in(own, 4), (amount // 2,), 0, 1 << 20) % (margin + 1)
    sizes = sizes.at[donor].add(-moved).at[receiver].add(moved)
    members = jnp.searchsorted(jnp.cumsum(sizes), jnp.arange(rows * top), side="right").astype(jnp.int32)
    table = members.reshape(top, rows).T
    table = table[jax.random.permutation(jax.random.fold_in(own, 1), rows)]
    offset_by = jax.random.randint(jax.random.fold_in(own, 2), (rows, 1), 0, top)
    return jnp.take_along_axis(table, (jnp.arange(top)[None, :] + offset_by) % top, axis=1)


def shares(number_of, total, reach, lean, full):
    portions = [(1 << 20) // math.isqrt(grade ** lean) + 1 for grade in range(1, number_of + 1)]
    largest = reach if full else min(reach, max(-(-total // number_of), total * portions[0] // sum(portions)))
    least = 1 if total - largest >= number_of - 1 else 0
    holding, surplus = [largest] + [least] * (number_of - 1), total - largest - least * (number_of - 1)
    while surplus > 0:
        candidates = [i for i in range(1, number_of) if holding[i] < largest] or [i for i in range(1, number_of) if holding[i] < reach]
        pool, left = sum([portions[i] for i in candidates]), surplus
        for i in candidates:
            extra = min(reach - holding[i], max(1, left * portions[i] // pool), surplus)
            holding[i] = holding[i] + extra
            surplus = surplus - extra
    return np.array(holding)


def noise(rng, extent, width, reach, pieces=(), kind=jnp.bfloat16):
    entries = width * jax.random.normal(rng, extent, jnp.float32)
    if pieces:
        entries = entries * steps_of(rng, extent, pieces, -0.22, 0.18)
    return jnp.clip(entries, -reach, reach).astype(kind)


def setup_inputs(seed: int = 0, part: int = 0) -> dict:
    seeds = jax.random.split(jax.random.key(seed), 13)
    part_keys = jax.random.split(jax.random.fold_in(seeds[12], part), 13)
    queries = draw_queries(jax.random.fold_in(jax.random.fold_in(seeds[12], part), 71), part)
    token_key_heads = draw_token_key_heads(jax.random.fold_in(jax.random.fold_in(seeds[12], part), 71), part)
    token_value_heads = noise(part_keys[2], (SLAB_TOKENS, KEY_VALUE_HEADS * HEAD_SIZE), 1.0, 6.0, ((0, 16),))
    residual = draw_residual(jax.random.fold_in(jax.random.fold_in(seeds[12], part), 71), part)
    out_weight = noise(seeds[4], (QUERY_HEADS * HEAD_SIZE, D), (QUERY_HEADS * HEAD_SIZE) ** -0.5, 0.125, ((0, 16),))
    norm_gain = jnp.clip(1.0 + 0.1 * jax.random.normal(seeds[5], (D,), jnp.float32), 0.5, 1.5).astype(jnp.bfloat16)
    w_gate = noise(seeds[6], (EXPERTS, D, FF), D ** -0.5, 0.1875, ((0, 16),))
    w_up = noise(seeds[7], (EXPERTS, D, FF), D ** -0.5, 0.1875, ((0, 16),))
    w_down = noise(seeds[8], (EXPERTS, FF, D), FF ** -0.5, 0.3125, ((0, 16),))
    expert_ids_keys = jax.random.split(jax.random.fold_in(part_keys[9], 1), SLAB_TOKENS // TOK_DEV)
    expert_ids_turns = jax.random.permutation(jax.random.fold_in(part_keys[9], 3), SLAB_TOKENS // TOK_DEV)
    expert_ids = jax.vmap(lambda own, number: assign_block(jax.random.fold_in(part_keys[9], 2), own, number, TOK_DEV, EXPERTS, TOP, SLOT, 2))(expert_ids_keys, expert_ids_turns).reshape((SLAB_TOKENS, TOP))
    gate_weights = jnp.clip(0.05 + 0.25 * jax.random.uniform(part_keys[10], (SLAB_TOKENS, TOP), jnp.float32) ** steps_of(part_keys[10], (SLAB_TOKENS, TOP), ((0, 16),), -0.2, 0.2), 0.05, 0.3)
    doc_of_block = jnp.searchsorted(jnp.cumsum(uneven(part_keys[11], DOCS, N_SEQ, MOST_BLK, 0)), jnp.arange(N_SEQ), side="right").astype(jnp.int32)
    return dict(queries=queries, token_key_heads=token_key_heads, token_value_heads=token_value_heads, residual=residual, out_weight=out_weight, norm_gain=norm_gain, w_gate=w_gate, w_up=w_up, w_down=w_down, expert_ids=expert_ids, gate_weights=gate_weights, doc_of_block=doc_of_block)


def reference(queries, token_key_heads, token_value_heads, residual, out_weight, norm_gain, w_gate, w_up, w_down, expert_ids, gate_weights, doc_of_block):
    heads_per_group = QUERY_HEADS // KEY_VALUE_HEADS
    query_every_head = queries.reshape(SLAB_TOKENS, KEY_VALUE_HEADS, heads_per_group, HEAD_SIZE).astype(jnp.float32)
    key_every_head = token_key_heads.reshape(SLAB_TOKENS, KEY_VALUE_HEADS, HEAD_SIZE).astype(jnp.float32)
    value_every_head = token_value_heads.reshape(SLAB_TOKENS, KEY_VALUE_HEADS, HEAD_SIZE).astype(jnp.float32)
    key_pos = jnp.arange(SLAB_TOKENS, dtype=jnp.int32)
    key_block = key_pos // TOK_DEV
    key_doc = doc_of_block[key_block]
    factor = 1.0 / HEAD_SIZE ** 0.5

    def attend_block(block):
        query_block = lax.dynamic_slice_in_dim(query_every_head, (block * TOK_DEV).astype(jnp.int32), TOK_DEV, 0)
        query_pos = block * TOK_DEV + jnp.arange(TOK_DEV, dtype=jnp.int32)
        allowed = (key_block <= block) & ((key_doc == doc_of_block[block]) | (key_block == 0))
        visible = allowed[None, :] & (key_pos[None, :] <= query_pos[:, None])
        scores = jnp.einsum('tkgd,skd->kgts', query_block, key_every_head) * factor
        scores = jnp.where(visible, scores, -1e+30)
        top_score = lax.optimization_barrier(jnp.max(scores, axis=-1, keepdims=True))
        terms = jnp.where(visible, jnp.exp(scores - top_score), 0.0)
        denom = lax.optimization_barrier(jnp.sum(terms, axis=-1))
        probs = lax.optimization_barrier(terms.astype(jnp.bfloat16)).astype(jnp.float32)
        summed = jnp.einsum('kgts,skd->tkgd', probs, value_every_head)
        result = summed / jnp.transpose(denom, (2, 0, 1))[..., None]
        return result.reshape(TOK_DEV, QUERY_HEADS * HEAD_SIZE).astype(jnp.bfloat16)
    attention = lax.map(attend_block, jnp.arange(N_SEQ, dtype=jnp.int32)).reshape(SLAB_TOKENS, QUERY_HEADS * HEAD_SIZE)
    hidden_state = residual.astype(jnp.float32) + jnp.dot(attention, out_weight, preferred_element_type=jnp.float32)
    mean_square = lax.optimization_barrier(jnp.mean(hidden_state * hidden_state, axis=-1, keepdims=True))
    normed = (hidden_state * lax.rsqrt(mean_square + 1e-06) * norm_gain.astype(jnp.float32)).astype(jnp.bfloat16)

    def one_expert(running, expert):
        gate_part = jnp.dot(normed, w_gate[expert], preferred_element_type=jnp.float32)
        up_part = jnp.dot(normed, w_up[expert], preferred_element_type=jnp.float32)
        activated = (jax.nn.silu(gate_part) * up_part).astype(jnp.bfloat16)
        produced = jnp.dot(activated, w_down[expert], preferred_element_type=jnp.float32).astype(jnp.bfloat16)
        weight = lax.optimization_barrier(jnp.sum(jnp.where(expert_ids == expert, gate_weights, 0.0), axis=-1))
        return (running + weight[:, None] * produced.astype(jnp.float32), None)
    expert_mix, _ = lax.scan(one_expert, jnp.zeros((SLAB_TOKENS, D), jnp.float32), jnp.arange(EXPERTS, dtype=jnp.int32))
    return (attention, hidden_state.astype(jnp.bfloat16), expert_mix.astype(jnp.bfloat16))
```

```python
import functools
import math

import jax
import jax.numpy as jnp
from jax import lax
from jax.experimental import pallas as pl
from jax.experimental.pallas import tpu as pltpu
from jax.sharding import PartitionSpec as P

QUERY_HEADS = 16
KEY_VALUE_HEADS = 2
HEAD_SIZE = 128
MOST_BLK = 8
GROUP = QUERY_HEADS // KEY_VALUE_HEADS
F32 = jnp.float32
BF16 = jnp.bfloat16
VMEM_LIMIT = 48 * 1024 * 1024


def chip_at(place, chips):
    half = chips // 2
    return jnp.where(place < half, 2 * place, 2 * (chips - 1 - place) + 1)


def place_of(chip, chips):
    return jnp.where(chip % 2 == 0, chip // 2, chips - 1 - chip // 2)


def ring_steps(chips):
    order = [2 * i for i in range(chips // 2)] + [2 * i + 1 for i in reversed(range(chips // 2))]
    forward = [
        (2 * order[i] + k, 2 * order[(i + 1) % chips] + k) for i in range(chips) for k in range(2)
    ]
    return forward, [(b, a) for a, b in forward]


def core_step(devices):
    return [(i, i ^ 1) for i in range(devices)]


def piece_places(chips):
    places = [0]
    for j in range(1, chips // 2):
        places += [-j, j]
    return places + [chips // 2]


def ring_gather(piece, devices):
    chips = devices // 2
    forward, backward = ring_steps(chips)
    rows = piece.shape[0]
    cut = rows // 2 // 16 * 16
    pieces = {0: piece}
    ahead = behind = piece
    for j in range(1, chips // 2):
        ahead = lax.ppermute(ahead, "seq", forward)
        behind = lax.ppermute(behind, "seq", backward)
        pieces[-j], pieces[j] = ahead, behind
    far = (
        lax.ppermute(ahead[:cut], "seq", forward),
        lax.ppermute(behind[cut:], "seq", backward),
    )
    return pieces, far


def gather_all(piece, devices):
    chips = devices // 2
    pieces, far = ring_gather(piece, devices)
    pieces[chips // 2] = jnp.concatenate(far, axis=0)
    swap = core_step(devices)
    return [(pieces[d], lax.ppermute(pieces[d], "seq", swap)) for d in piece_places(chips)]


def block_of(own, offset, other, devices):
    chips = devices // 2
    place = (place_of(own // 2, chips) + offset + chips) % chips
    return chip_at(place, chips) * 2 + (own % 2 if other == 0 else 1 - own % 2)


def attend_kernel(offsets, devices, own_ref, doc_ref, q_ref, *refs):
    count = 2 * len(offsets)
    kv_refs = refs[:count]
    out_ref, keys, values, bias = refs[count:]
    rows = q_ref.shape[0]
    width = KEY_VALUE_HEADS * HEAD_SIZE
    window = keys.shape[1]
    own = own_ref[0]
    own_doc = doc_ref[own]
    lane = lax.broadcasted_iota(jnp.int32, (window, HEAD_SIZE), 1)
    one_column = jnp.where(lane == 0, 1.0, 0.0).astype(BF16)
    for g in range(KEY_VALUE_HEADS):
        keys[g] = jnp.zeros((window, HEAD_SIZE), BF16)
        values[g, :, :HEAD_SIZE] = jnp.zeros((window, HEAD_SIZE), BF16)
        values[g, :, HEAD_SIZE:] = one_column

    def put(ref, slot):
        start = pl.multiple_of(slot * rows, rows)
        for g in range(KEY_VALUE_HEADS):
            keys[g, pl.ds(start, rows), :] = ref[:rows, g * HEAD_SIZE : (g + 1) * HEAD_SIZE]
            values[g, pl.ds(start, rows), :HEAD_SIZE] = ref[
                :rows, width + g * HEAD_SIZE : width + (g + 1) * HEAD_SIZE
            ]

    put(kv_refs[0], 0)
    slot = jnp.int32(1)
    for i in range(1, count):
        block = block_of(own, offsets[i // 2], i % 2, devices)
        seen = (block < own) & ((block == 0) | (doc_ref[block] == own_doc))
        pl.when(seen)(functools.partial(put, kv_refs[i], slot))
        slot = slot + seen.astype(jnp.int32)
    query_row = lax.broadcasted_iota(jnp.int32, (rows, rows), 0)
    key_row = lax.broadcasted_iota(jnp.int32, (rows, rows), 1)
    bias[:, :rows] = jnp.where(key_row <= query_row, 0.0, -1e30)
    later_row = lax.broadcasted_iota(jnp.int32, (rows, window - rows), 1)
    bias[:, rows:] = jnp.where(later_row < (slot - 1) * rows, 0.0, -1e30)
    factor = math.log2(math.e) / HEAD_SIZE**0.5
    heads = 4
    for first in range(0, QUERY_HEADS, heads):
        g = first // GROUP
        q = jnp.concatenate(
            [
                q_ref[:, (first + h) * HEAD_SIZE : (first + h + 1) * HEAD_SIZE]
                for h in range(heads)
            ],
            axis=0,
        )
        scores = lax.dot_general(
            q, keys[g], (((1,), (1,)), ((), ())), preferred_element_type=F32
        )
        scores = scores.reshape(heads, rows, window) * factor + bias[...][None]
        top = jnp.max(scores, axis=-1, keepdims=True)
        probs = jnp.exp2(scores - top).astype(BF16).reshape(heads * rows, window)
        summed = jnp.dot(probs, values[g], preferred_element_type=F32)
        result = (summed[:, :HEAD_SIZE] / summed[:, HEAD_SIZE : HEAD_SIZE + 1]).astype(BF16)
        for h in range(heads):
            out_ref[:, (first + h) * HEAD_SIZE : (first + h + 1) * HEAD_SIZE] = result[
                h * rows : (h + 1) * rows
            ]


def attend(own, docs, queries, kv_pieces, devices):
    rows = queries.shape[0]
    offsets = piece_places(devices // 2)
    window = (min(MOST_BLK, devices) + 1) * rows
    flat = [p for pair in kv_pieces for p in pair]
    vmem = pl.BlockSpec(memory_space=pltpu.VMEM)
    smem = pl.BlockSpec(memory_space=pltpu.SMEM)
    return pl.pallas_call(
        functools.partial(attend_kernel, offsets, devices),
        out_shape=jax.ShapeDtypeStruct(queries.shape, BF16),
        in_specs=[smem, smem, vmem] + [vmem] * len(flat),
        out_specs=vmem,
        scratch_shapes=[
            pltpu.VMEM((KEY_VALUE_HEADS, window, HEAD_SIZE), BF16),
            pltpu.VMEM((KEY_VALUE_HEADS, window, 2 * HEAD_SIZE), BF16),
            pltpu.VMEM((rows, window), F32),
        ],
        compiler_params=pltpu.CompilerParams(vmem_limit_bytes=VMEM_LIMIT),
        cost_estimate=pl.CostEstimate(
            flops=4 * QUERY_HEADS * rows * window * HEAD_SIZE,
            bytes_accessed=8 * 2**20,
            transcendentals=QUERY_HEADS * rows * window,
        ),
        name="attend",
    )(own, docs, queries, *flat)


def project_kernel(offsets, devices, own_ref, att_ref, res_ref, gain_ref, *refs):
    count = 2 * len(offsets)
    w_refs = refs[:count]
    hidden_ref, normed_ref, weight, sems = refs[count:]
    own = own_ref[0]
    rows = w_refs[0].shape[0]
    copies = []
    for i in range(count):
        block = block_of(own, offsets[i // 2], i % 2, devices)
        copies.append(
            pltpu.make_async_copy(
                w_refs[i],
                weight.at[pl.ds(pl.multiple_of(block * rows, rows), rows), :],
                sems.at[i],
            )
        )
        copies[-1].start()
    for c in copies:
        c.wait()
    hidden = res_ref[...].astype(F32) + jnp.dot(
        att_ref[...], weight[...], preferred_element_type=F32
    )
    hidden_ref[...] = hidden.astype(BF16)
    mean_square = jnp.mean(hidden * hidden, axis=-1, keepdims=True)
    normed_ref[...] = (
        hidden * lax.rsqrt(mean_square + 1e-06) * gain_ref[...].astype(F32)
    ).astype(BF16)


def project(own, attention, residual, gain, w_pieces, devices):
    offsets = piece_places(devices // 2)
    flat = [p for pair in w_pieces for p in pair]
    vmem = pl.BlockSpec(memory_space=pltpu.VMEM)
    smem = pl.BlockSpec(memory_space=pltpu.SMEM)
    hbm = pl.BlockSpec(memory_space=pl.ANY)
    total = flat[0].shape[0] * devices
    return pl.pallas_call(
        functools.partial(project_kernel, offsets, devices),
        out_shape=(
            jax.ShapeDtypeStruct(residual.shape, BF16),
            jax.ShapeDtypeStruct(residual.shape, BF16),
        ),
        in_specs=[smem, vmem, vmem, vmem] + [hbm] * len(flat),
        out_specs=(vmem, vmem),
        scratch_shapes=[
            pltpu.VMEM((total, residual.shape[1]), BF16),
            pltpu.SemaphoreType.DMA((len(flat),)),
        ],
        compiler_params=pltpu.CompilerParams(vmem_limit_bytes=VMEM_LIMIT),
        cost_estimate=pl.CostEstimate(
            flops=2 * residual.shape[0] * total * residual.shape[1],
            bytes_accessed=6 * 2**20,
            transcendentals=0,
        ),
        name="project",
    )(own, attention, residual, gain.reshape(1, -1), *flat)


def expert_kernel(first, count, scale_ref, gate_ref, up_ref, down_ref, *refs):
    x_refs, out_refs = refs[:count], refs[count:]
    rows = x_refs[0].shape[0]
    x = jnp.concatenate([r[...] for r in x_refs], axis=0)
    gate_part = jnp.dot(x, gate_ref[...], preferred_element_type=F32)
    up_part = jnp.dot(x, up_ref[...], preferred_element_type=F32)
    activated = (gate_part / (1.0 + jnp.exp(-gate_part)) * up_part).astype(BF16)
    produced = jnp.dot(activated, down_ref[...], preferred_element_type=F32)
    for i in range(count):
        out_refs[i][...] = (
            produced[i * rows : (i + 1) * rows] * scale_ref[:, first + i : first + i + 1]
        ).astype(BF16)


def expert(scale, gate_proj, up_proj, down_proj, first, pieces):
    vmem = pl.BlockSpec(memory_space=pltpu.VMEM)
    count = len(pieces)
    shape = jax.ShapeDtypeStruct(pieces[0].shape, BF16)
    rows = count * shape.shape[0]
    return pl.pallas_call(
        functools.partial(expert_kernel, first, count),
        out_shape=(shape,) * count,
        in_specs=[vmem] * (4 + count),
        out_specs=(vmem,) * count,
        compiler_params=pltpu.CompilerParams(vmem_limit_bytes=VMEM_LIMIT),
        cost_estimate=pl.CostEstimate(
            flops=6 * rows * gate_proj.shape[0] * gate_proj.shape[1],
            bytes_accessed=4 * 2**20,
            transcendentals=rows * gate_proj.shape[1],
        ),
        name="expert",
    )(scale, gate_proj, up_proj, down_proj, *pieces)


def added(*terms):
    return functools.reduce(lambda a, b: a + b, [t.astype(F32) for t in terms])


def ring_scatter_sum(parts, devices):
    chips = devices // 2
    half = chips // 2
    forward, backward = ring_steps(chips)
    swap = core_step(devices)
    terms = {d: (own, lax.ppermute(other, "seq", swap)) for d, (own, other) in parts.items()}
    far = added(*terms[half]).astype(BF16)
    cut = far.shape[0] // 2
    ahead = lax.ppermute(far[:cut], "seq", forward)
    behind = lax.ppermute(far[cut:], "seq", backward)
    pad = jnp.zeros((cut, far.shape[1]), BF16)
    ahead = jnp.concatenate([ahead, pad], axis=0)
    behind = jnp.concatenate([pad, behind], axis=0)
    for j in range(half - 1, 0, -1):
        ahead = lax.ppermute(added(ahead, *terms[j]).astype(BF16), "seq", forward)
        behind = lax.ppermute(added(behind, *terms[-j]).astype(BF16), "seq", backward)
    return added(ahead, behind, *terms[0]).astype(BF16)


def shards(
    queries,
    token_key_heads,
    token_value_heads,
    residual,
    out_weight,
    norm_gain,
    w_gate,
    w_up,
    w_down,
    expert_ids,
    gate_weights,
    doc_of_block,
):
    devices = lax.axis_size("seq")
    chips = devices // 2
    rows = queries.shape[0]
    own = lax.axis_index("seq").astype(jnp.int32)
    own_ref = own.reshape(1)

    experts = jnp.arange(devices, dtype=jnp.int32)
    by_expert = jnp.sum(
        jnp.where(expert_ids[None] == experts[:, None, None], gate_weights[None], 0.0), axis=-1
    )
    high = by_expert.astype(BF16)
    low = (by_expert - high.astype(F32)).astype(BF16)
    kv_width = 2 * token_key_heads.shape[1]
    split = jnp.concatenate([high, low], axis=0).reshape(-1, kv_width)
    extra = split.shape[0]
    padded = -(-extra // 16) * 16
    split = jnp.pad(split, ((0, padded - extra), (0, 0)))
    packed = jnp.concatenate(
        [jnp.concatenate([token_key_heads, token_value_heads], axis=1), split], axis=0
    )
    kv_pieces = gather_all(packed, devices)
    w_pieces = gather_all(out_weight, devices)

    attention = attend(own_ref, doc_of_block, queries, kv_pieces, devices)
    hidden, normed = project(own_ref, attention, residual, norm_gain, w_pieces, devices)

    scales = jnp.stack([p[rows : rows + extra] for pair in kv_pieces for p in pair])
    scales = scales.reshape(devices, 2, devices, rows)
    scales = lax.dynamic_index_in_dim(scales, own, axis=2, keepdims=False).astype(F32)
    scales = jnp.transpose(scales[:, 0] + scales[:, 1])

    tokens = gather_all(normed, devices)
    offsets = piece_places(chips)
    groups = [[0]] + [[i, i + 1] for i in range(1, chips - 1, 2)] + [[chips - 1]]
    parts = {}
    for group in groups:
        pieces = [p for i in group for p in tokens[i]]
        outs = expert(scales, w_gate[0], w_up[0], w_down[0], 2 * group[0], pieces)
        for n, i in enumerate(group):
            parts[offsets[i]] = (outs[2 * n], outs[2 * n + 1])
    mix = ring_scatter_sum(parts, devices)
    return (attention, hidden, mix)


def solution(mesh):
    in_specs = (
        P(("pack", "seq"), None),
        P(("pack", "seq"), None),
        P(("pack", "seq"), None),
        P(("pack", "seq"), None),
        P("seq", None),
        P(),
        P("seq", None, None),
        P("seq", None, None),
        P("seq", None, None),
        P(("pack", "seq"), None),
        P(("pack", "seq"), None),
        P("pack"),
    )
    out_specs = (P(("pack", "seq"), None), P(("pack", "seq"), None), P(("pack", "seq"), None))
    return jax.shard_map(shards, mesh=mesh, in_specs=in_specs, out_specs=out_specs, check_vma=False)
```

```python
import functools
import math

import jax
import jax.numpy as jnp
from jax import lax
from jax.experimental import pallas as pl
from jax.experimental.pallas import tpu as pltpu
from jax.sharding import PartitionSpec as P

QUERY_HEADS = 16
KEY_VALUE_HEADS = 2
HEAD_SIZE = 128
MOST_BLK = 8
GROUP = QUERY_HEADS // KEY_VALUE_HEADS
F32 = jnp.float32
BF16 = jnp.bfloat16
VMEM_LIMIT = 60 * 1024 * 1024
VMEM = pl.BlockSpec(memory_space=pltpu.VMEM)
SMEM = pl.BlockSpec(memory_space=pltpu.SMEM)
HBM = pl.BlockSpec(memory_space=pl.ANY)
PARAMS = pltpu.CompilerParams(vmem_limit_bytes=VMEM_LIMIT)


def ring_steps(chips):
    order = [2 * i for i in range(chips // 2)] + [2 * i + 1 for i in reversed(range(chips // 2))]
    steps = []
    for i in range(chips):
        steps.append((2 * order[i], 2 * order[(i + 1) % chips]))
        steps.append((2 * order[i] + 1, 2 * order[i - 1] + 1))
    return steps


def swap_steps(devices):
    return [(i, i ^ 1) for i in range(devices)]


def piece_groups(chips):
    groups = [[(0, 0), (0, 1)]]
    for j in range(1, chips // 2):
        groups.append([(-j, 0), (-j, 1), (j, 1), (j, 0)])
    return groups + [[(-(chips // 2), 0), (chips // 2, 1)]]


def piece_names(devices):
    return [name for group in piece_groups(devices // 2) for name in group]


def block_of(own, name, devices):
    chips = devices // 2
    chip, core = own // 2, own % 2
    place = jnp.where(chip % 2 == 0, chip // 2, chips - 1 - chip // 2)
    place = (place + jnp.where(core == 0, name[0], -name[0]) + chips) % chips
    chip = jnp.where(place < chips // 2, 2 * place, 2 * (chips - 1 - place) + 1)
    return 2 * chip + (core if name[1] == 0 else 1 - core)


def ring_gather(piece, devices):
    half = devices // 4
    ring, swap = ring_steps(devices // 2), swap_steps(devices)
    other = lax.ppermute(piece, "seq", swap)
    pieces = {(0, 0): piece, (0, 1): other}
    first, second = piece, other
    for j in range(1, half + 1):
        first = lax.ppermute(first, "seq", ring)
        pieces[-j, 0], pieces[j, 1] = first, lax.ppermute(first, "seq", swap)
        if j < half:
            second = lax.ppermute(second, "seq", ring)
            pieces[-j, 1], pieces[j, 0] = second, lax.ppermute(second, "seq", swap)
    return pieces


def added(*terms):
    return functools.reduce(lambda a, b: a + b, [t.astype(F32) for t in terms])


def ring_scatter_sum(kept, sent, devices):
    half = devices // 4
    back = [(b, a) for a, b in ring_steps(devices // 2)]
    swap = swap_steps(devices)
    got = {j: lax.ppermute(sent[j], "seq", swap) for j in range(half, 0, -1)}
    rows = sent[half].shape[0]
    first, second = [], []
    for j in range(half, 0, -1):
        first = [lax.ppermute(added(kept[j][:rows], got[j][:rows], *first).astype(BF16), "seq", back)]
        if j < half:
            terms = added(kept[j][rows:], got[j][rows:], *second)
            second = [lax.ppermute(terms.astype(BF16), "seq", back)]
    last = lax.ppermute(added(kept[0][rows:], *second).astype(BF16), "seq", swap)
    return added(kept[0][:rows], last, *first).astype(BF16)


def pack_kernel(devices, key_ref, value_ref, id_ref, weight_ref, out_ref):
    rows, width = key_ref.shape
    out_ref[:rows, :width] = key_ref[...]
    out_ref[:rows, width:] = value_ref[...]
    ids = jnp.transpose(id_ref[...].astype(F32))
    weights = jnp.transpose(weight_ref[...])
    by_expert = [
        jnp.sum(jnp.where(ids == e, weights, 0.0), axis=0, keepdims=True) for e in range(devices)
    ]
    in_row = 2 * width // rows
    lines = []
    for first in range(0, devices, in_row):
        lines.append(jnp.concatenate(by_expert[first : first + in_row], axis=1))
    high = [line.astype(BF16).astype(F32) for line in lines]
    low = [line - h for line, h in zip(lines, high)]
    extra = out_ref.shape[0] - rows
    filled = 2 * len(lines)
    if extra > filled:
        low.append(jnp.zeros((extra - filled, 2 * width), F32))
    out_ref[rows:, :] = jnp.concatenate(high + low, axis=0).astype(BF16)


def pack(keys, values, ids, weights, devices):
    rows, width = keys.shape
    lines = 2 * (devices * rows // (2 * width))
    return pl.pallas_call(
        functools.partial(pack_kernel, devices),
        out_shape=jax.ShapeDtypeStruct((rows + -(-lines // 16) * 16, 2 * width), BF16),
        in_specs=[VMEM] * 4,
        out_specs=VMEM,
        compiler_params=PARAMS,
        cost_estimate=pl.CostEstimate(flops=10**6, bytes_accessed=2**19, transcendentals=0),
        name="pack",
    )(keys, values, ids, weights)


def attend_kernel(devices, own_ref, doc_ref, q_ref, *refs):
    names = piece_names(devices)
    kv_refs = refs[: len(names)]
    out_ref, scale_ref, keys, values, bias, lines, sems = refs[len(names) :]
    rows = q_ref.shape[0]
    width = KEY_VALUE_HEADS * HEAD_SIZE
    window = keys.shape[1]
    own = own_ref[0]
    own_doc = doc_ref[own]

    def copies(i, slot):
        start = pl.multiple_of(slot * rows, rows)
        made = []
        for g in range(KEY_VALUE_HEADS):
            for part, buffer in enumerate((keys, values)):
                column = part * width + g * HEAD_SIZE
                made.append(
                    pltpu.make_async_copy(
                        kv_refs[i].at[pl.ds(0, rows), pl.ds(column, HEAD_SIZE)],
                        buffer.at[g, pl.ds(start, rows), pl.ds(0, HEAD_SIZE)],
                        sems.at[i, len(made)],
                    )
                )
        return made

    def line_copy(i):
        extra = lines.shape[1]
        return pltpu.make_async_copy(
            kv_refs[i].at[pl.ds(rows, extra), :], lines.at[i], sems.at[i, 4]
        )

    for i in range(len(names)):
        line_copy(i).start()
    slots, seen = [jnp.int32(0)], [True]
    for c in copies(0, 0):
        c.start()
    filled = jnp.int32(1)
    for i in range(1, len(names)):
        block = block_of(own, names[i], devices)
        shown = (block < own) & ((block == 0) | (doc_ref[block] == own_doc))
        slots.append(filled)
        seen.append(shown)

        @pl.when(shown)
        def _(i=i, slot=filled):
            for c in copies(i, slot):
                c.start()

        filled = filled + shown.astype(jnp.int32)

    for s in range(1, window // rows):

        @pl.when(s >= filled)
        def _(s=s):
            for g in range(KEY_VALUE_HEADS):
                blank = jnp.zeros((rows, HEAD_SIZE), BF16)
                keys[g, s * rows : (s + 1) * rows, :] = blank
                values[g, s * rows : (s + 1) * rows, :HEAD_SIZE] = blank

    lane = lax.broadcasted_iota(jnp.int32, (window, HEAD_SIZE), 1)
    one_column = jnp.where(lane == 0, 1.0, 0.0).astype(BF16)
    for g in range(KEY_VALUE_HEADS):
        values[g, :, HEAD_SIZE:] = one_column
    query_row = lax.broadcasted_iota(jnp.int32, (rows, rows), 0)
    key_row = lax.broadcasted_iota(jnp.int32, (rows, rows), 1)
    bias[:, :rows] = jnp.where(key_row <= query_row, 0.0, -1e30)
    later_row = lax.broadcasted_iota(jnp.int32, (rows, window - rows), 1)
    bias[:, rows:] = jnp.where(later_row < (filled - 1) * rows, 0.0, -1e30)

    for i in range(len(names)):
        line_copy(i).wait()
    count = devices * rows // (2 * width)
    in_row = 2 * width // rows
    line = lax.broadcasted_iota(jnp.int32, (lines.shape[1], 2 * width), 0)
    wanted = (line == own // in_row) | (line == count + own // in_row)
    picked = []
    for i in range(len(names)):
        both = jnp.sum(jnp.where(wanted, lines[i].astype(F32), 0.0), axis=0, keepdims=True)
        picked.append(
            sum(
                jnp.where(own % in_row == n, both[:, n * rows : (n + 1) * rows], 0.0)
                for n in range(in_row)
            )
        )
    picked.append(jnp.zeros((rows - len(names), rows), F32))
    scale_ref[...] = jnp.transpose(jnp.concatenate(picked, axis=0))

    for i in range(len(names)):
        if i == 0:
            for c in copies(0, 0):
                c.wait()
        else:

            @pl.when(seen[i])
            def _(i=i):
                for c in copies(i, slots[i]):
                    c.wait()

    factor = math.log2(math.e) / HEAD_SIZE**0.5
    heads = 4
    for first in range(0, QUERY_HEADS, heads):
        g = first // GROUP
        q = jnp.concatenate(
            [
                q_ref[:, (first + h) * HEAD_SIZE : (first + h + 1) * HEAD_SIZE]
                for h in range(heads)
            ],
            axis=0,
        )
        scores = lax.dot_general(
            q, keys[g], (((1,), (1,)), ((), ())), preferred_element_type=F32
        )
        scores = scores.reshape(heads, rows, window) * factor + bias[...][None]
        top = jnp.max(scores, axis=-1, keepdims=True)
        probs = jnp.exp2(scores - top).astype(BF16).reshape(heads * rows, window)
        summed = jnp.dot(probs, values[g], preferred_element_type=F32)
        result = (summed[:, :HEAD_SIZE] / summed[:, HEAD_SIZE : HEAD_SIZE + 1]).astype(BF16)
        for h in range(heads):
            out_ref[:, (first + h) * HEAD_SIZE : (first + h + 1) * HEAD_SIZE] = result[
                h * rows : (h + 1) * rows
            ]


def attend(own, docs, queries, kv_pieces, devices):
    rows = queries.shape[0]
    window = (min(MOST_BLK, devices) + 1) * rows
    names = piece_names(devices)
    packed = kv_pieces[names[0]]
    return pl.pallas_call(
        functools.partial(attend_kernel, devices),
        out_shape=(
            jax.ShapeDtypeStruct(queries.shape, BF16),
            jax.ShapeDtypeStruct((rows, rows), F32),
        ),
        in_specs=[SMEM, SMEM, VMEM] + [HBM] * len(names),
        out_specs=(VMEM, VMEM),
        scratch_shapes=[
            pltpu.VMEM((KEY_VALUE_HEADS, window, HEAD_SIZE), BF16),
            pltpu.VMEM((KEY_VALUE_HEADS, window, 2 * HEAD_SIZE), BF16),
            pltpu.VMEM((rows, window), F32),
            pltpu.VMEM((len(names), packed.shape[0] - rows, packed.shape[1]), BF16),
            pltpu.SemaphoreType.DMA((len(names), 5)),
        ],
        compiler_params=PARAMS,
        cost_estimate=pl.CostEstimate(
            flops=4 * QUERY_HEADS * rows * window * HEAD_SIZE,
            bytes_accessed=8 * 2**20,
            transcendentals=QUERY_HEADS * rows * window,
        ),
        name="attend",
    )(own, docs, queries, *[kv_pieces[n] for n in names])


def project_kernel(devices, own_ref, att_ref, res_ref, gain_ref, *refs):
    names = piece_names(devices)
    w_refs = refs[: len(names)]
    hidden_ref, normed_ref, weight, sems = refs[len(names) :]
    own = own_ref[0]
    rows = w_refs[0].shape[0]
    copies = []
    for i, name in enumerate(names):
        start = pl.multiple_of(block_of(own, name, devices) * rows, rows)
        copies.append(
            pltpu.make_async_copy(w_refs[i], weight.at[pl.ds(start, rows), :], sems.at[i])
        )
        copies[-1].start()
    for c in copies:
        c.wait()
    hidden = res_ref[...].astype(F32) + jnp.dot(
        att_ref[...], weight[...], preferred_element_type=F32
    )
    hidden_ref[...] = hidden.astype(BF16)
    mean_square = jnp.mean(hidden * hidden, axis=-1, keepdims=True)
    normed_ref[...] = (
        hidden * lax.rsqrt(mean_square + 1e-06) * gain_ref[...].astype(F32)
    ).astype(BF16)


def project(own, attention, residual, gain, w_pieces, devices):
    names = piece_names(devices)
    total = w_pieces[names[0]].shape[0] * devices
    shape = jax.ShapeDtypeStruct(residual.shape, BF16)
    return pl.pallas_call(
        functools.partial(project_kernel, devices),
        out_shape=(shape, shape),
        in_specs=[SMEM, VMEM, VMEM, VMEM] + [HBM] * len(names),
        out_specs=(VMEM, VMEM),
        scratch_shapes=[
            pltpu.VMEM((total, residual.shape[1]), BF16),
            pltpu.SemaphoreType.DMA((len(names),)),
        ],
        compiler_params=PARAMS,
        cost_estimate=pl.CostEstimate(
            flops=2 * residual.shape[0] * total * residual.shape[1],
            bytes_accessed=6 * 2**20,
            transcendentals=0,
        ),
        name="project",
    )(own, attention, residual, gain.reshape(1, -1), *[w_pieces[n] for n in names])


def expert_kernel(first, count, scale_ref, gate_ref, up_ref, down_ref, *refs):
    x_refs = refs[:count]
    kept_ref, sent_ref = refs[count : count + 2]
    rows = x_refs[0].shape[0]
    x = jnp.concatenate([r[...] for r in x_refs], axis=0)
    gate_part = jnp.dot(x, gate_ref[...], preferred_element_type=F32)
    up_part = jnp.dot(x, up_ref[...], preferred_element_type=F32)
    activated = (gate_part / (1.0 + jnp.exp(-gate_part)) * up_part).astype(BF16)
    produced = jnp.dot(activated, down_ref[...], preferred_element_type=F32)
    kept = kept_ref.shape[0] // rows
    for i in range(count):
        part = (
            produced[i * rows : (i + 1) * rows] * scale_ref[:, first + i : first + i + 1]
        ).astype(BF16)
        if i < kept:
            kept_ref[i * rows : (i + 1) * rows, :] = part
        else:
            sent_ref[(i - kept) * rows : (i - kept + 1) * rows, :] = part


def expert(scale, gate_proj, up_proj, down_proj, first, pieces, kept):
    count = len(pieces)
    rows, width = pieces[0].shape
    sent = max(count - kept, 1)
    return pl.pallas_call(
        functools.partial(expert_kernel, first, count),
        out_shape=(
            jax.ShapeDtypeStruct((kept * rows, width), BF16),
            jax.ShapeDtypeStruct((sent * rows if count > kept else 16, width), BF16),
        ),
        in_specs=[VMEM] * (4 + count),
        out_specs=(VMEM, VMEM),
        compiler_params=PARAMS,
        cost_estimate=pl.CostEstimate(
            flops=6 * count * rows * gate_proj.shape[0] * gate_proj.shape[1],
            bytes_accessed=4 * 2**20,
            transcendentals=count * rows * gate_proj.shape[1],
        ),
        name="expert",
    )(scale, gate_proj, up_proj, down_proj, *pieces)


def shards(
    queries,
    token_key_heads,
    token_value_heads,
    residual,
    out_weight,
    norm_gain,
    w_gate,
    w_up,
    w_down,
    expert_ids,
    gate_weights,
    doc_of_block,
):
    devices = lax.axis_size("seq")
    own = lax.axis_index("seq").astype(jnp.int32).reshape(1)
    packed = pack(token_key_heads, token_value_heads, expert_ids, gate_weights, devices)
    kv_pieces = ring_gather(packed, devices)
    w_pieces = ring_gather(out_weight, devices)
    attention, scales = attend(own, doc_of_block, queries, kv_pieces, devices)
    hidden, normed = project(own, attention, residual, norm_gain, w_pieces, devices)

    tokens = ring_gather(normed, devices)
    kept, sent = {}, {}
    first = 0
    for j, group in enumerate(piece_groups(devices // 2)):
        pieces = [tokens[name] for name in group]
        stays = len(pieces) if j == 0 else len(pieces) // 2
        kept[j], sent[j] = expert(scales, w_gate[0], w_up[0], w_down[0], first, pieces, stays)
        first += len(pieces)
    mix = ring_scatter_sum(kept, sent, devices)
    return (attention, hidden, mix)


def solution(mesh):
    in_specs = (
        P(("pack", "seq"), None),
        P(("pack", "seq"), None),
        P(("pack", "seq"), None),
        P(("pack", "seq"), None),
        P("seq", None),
        P(),
        P("seq", None, None),
        P("seq", None, None),
        P("seq", None, None),
        P(("pack", "seq"), None),
        P(("pack", "seq"), None),
        P("pack"),
    )
    out_specs = (P(("pack", "seq"), None), P(("pack", "seq"), None), P(("pack", "seq"), None))
    return jax.shard_map(shards, mesh=mesh, in_specs=in_specs, out_specs=out_specs, check_vma=False)
```

```python
import functools
import math

import jax
import jax.numpy as jnp
from jax import lax
from jax.experimental import pallas as pl
from jax.experimental.pallas import tpu as pltpu
from jax.sharding import PartitionSpec as P

QUERY_HEADS = 16
KEY_VALUE_HEADS = 2
HEAD_SIZE = 128
MOST_BLK = 8
GROUP = QUERY_HEADS // KEY_VALUE_HEADS
F32 = jnp.float32
BF16 = jnp.bfloat16
VMEM_LIMIT = 60 * 1024 * 1024
VMEM = pl.BlockSpec(memory_space=pltpu.VMEM)
SMEM = pl.BlockSpec(memory_space=pltpu.SMEM)
HBM = pl.BlockSpec(memory_space=pl.ANY)
PARAMS = pltpu.CompilerParams(vmem_limit_bytes=VMEM_LIMIT)


def ring_steps(chips):
    order = [2 * i for i in range(chips // 2)] + [2 * i + 1 for i in reversed(range(chips // 2))]
    steps, across = [], []
    for i in range(chips):
        ahead, behind = 2 * order[(i + 1) % chips], 2 * order[i - 1] + 1
        steps += [(2 * order[i], ahead), (2 * order[i] + 1, behind)]
        across += [(2 * order[i] + 1, ahead), (2 * order[i], behind)]
    return steps, across


def swap_steps(devices):
    return [(i, i ^ 1) for i in range(devices)]


def piece_groups(chips):
    groups = [[(0, 0), (0, 1)]]
    for j in range(1, chips // 2):
        groups.append([(-j, 0), (-j, 1), (j, 1), (j, 0)])
    return groups


def piece_names(devices):
    names = [name for group in piece_groups(devices // 2) for name in group]
    return names + [(-(devices // 4), 0), (-(devices // 4), 1)]


def source_of(name, tail, devices):
    half = devices // 4
    if name == (-half, 0):
        return name if tail else (half, 0)
    if name == (-half, 1):
        return (half, 1) if tail else name
    return name


def block_of(own, name, devices):
    chips = devices // 2
    chip, core = own // 2, own % 2
    place = jnp.where(chip % 2 == 0, chip // 2, chips - 1 - chip // 2)
    place = (place + jnp.where(core == 0, name[0], -name[0]) + chips) % chips
    chip = jnp.where(place < chips // 2, 2 * place, 2 * (chips - 1 - place) + 1)
    return 2 * chip + (core if name[1] == 0 else 1 - core)


def ring_gather(piece, cut, devices):
    half = devices // 4
    (ring, across), swap = ring_steps(devices // 2), swap_steps(devices)
    pieces = {(0, 0): piece}
    first = second = piece
    for j in range(1, half + 1):
        first = lax.ppermute(first if j < half else first[cut:], "seq", ring)
        second = lax.ppermute(
            second if j < half else second[:cut], "seq", across if j == 1 else ring
        )
        pieces[-j, 0], pieces[-j, 1] = first, second
    pieces[0, 1] = lax.ppermute(piece, "seq", swap)
    for j in range(1, half + 1):
        pieces[j, 1] = lax.ppermute(pieces[-j, 0], "seq", swap)
        pieces[j, 0] = lax.ppermute(pieces[-j, 1], "seq", swap)
    return pieces


def added(*terms):
    return functools.reduce(lambda a, b: a + b, [t.astype(F32) for t in terms])


def ring_scatter_sum(kept, sent, cut, devices):
    half = devices // 4
    ring, across = ring_steps(devices // 2)
    ring, across = [(b, a) for a, b in ring], [(b, a) for a, b in across]
    swap = swap_steps(devices)
    got = {j: lax.ppermute(sent[j], "seq", swap) for j in range(half, -1, -1)}
    rows = kept[0].shape[0]
    first, second = [], []
    for j in range(half, 0, -1):
        if j == half - 1:
            first = [jnp.pad(first[0], ((cut, 0), (0, 0)))]
            second = [jnp.pad(second[0], ((0, rows - cut), (0, 0)))]
        at = rows - cut if j == half else rows
        total = added(kept[j][:at], got[j][:at], *first).astype(BF16)
        _, received = lax.optimization_barrier((total, [got[j][at:], *second]))
        others = added(kept[j][at:], *received).astype(BF16)
        first = [lax.ppermute(total, "seq", ring)]
        second = [lax.ppermute(others, "seq", across if j == 1 else ring)]
    return added(kept[0], got[0], *first, *second).astype(BF16)


def pack_kernel(devices, key_ref, value_ref, id_ref, weight_ref, out_weight_ref, out_ref):
    rows, width = key_ref.shape
    out_ref[:rows, :width] = key_ref[...]
    out_ref[:rows, width:] = value_ref[...]
    ids, weights = id_ref[...], weight_ref[...]
    by_expert = [
        jnp.sum(jnp.where(ids == e, weights, 0.0), axis=0, keepdims=True) for e in range(devices)
    ]
    in_row = 2 * width // rows
    lines = []
    for first in range(0, devices, in_row):
        lines.append(jnp.concatenate(by_expert[first : first + in_row], axis=1))
    high = [line.astype(BF16).astype(F32) for line in lines]
    low = [line - h for line, h in zip(lines, high)]
    extra = line_rows(devices, rows, width)
    if extra > 2 * len(lines):
        low.append(jnp.zeros((extra - 2 * len(lines), 2 * width), F32))
    out_ref[rows : rows + extra, :] = jnp.concatenate(high + low, axis=0).astype(BF16)
    depth = out_weight_ref.shape[0]
    for n in range(out_weight_ref.shape[1] // (2 * width)):
        start = rows + extra + n * depth
        out_ref[start : start + depth, :] = out_weight_ref[:, 2 * width * n : 2 * width * (n + 1)]


def line_rows(devices, rows, width):
    lines = 2 * (devices * rows // (2 * width))
    return -(-lines // 16) * 16


def pack(keys, values, ids, weights, out_weight, devices):
    rows, width = keys.shape
    total = rows + line_rows(devices, rows, width)
    total += out_weight.shape[0] * out_weight.shape[1] // (2 * width)
    return pl.pallas_call(
        functools.partial(pack_kernel, devices),
        out_shape=jax.ShapeDtypeStruct((total, 2 * width), BF16),
        in_specs=[VMEM] * 5,
        out_specs=VMEM,
        compiler_params=PARAMS,
        cost_estimate=pl.CostEstimate(flops=10**6, bytes_accessed=2**20, transcendentals=0),
        name="pack",
    )(keys, values, jnp.transpose(ids), jnp.transpose(weights), out_weight)


def attend_kernel(devices, own_ref, doc_ref, q_ref, res_ref, gain_ref, *refs):
    names = piece_names(devices)
    head_refs, tail_refs = refs[: len(names)], refs[len(names) : 2 * len(names)]
    out_ref, scale_ref, hidden_ref, normed_ref = refs[2 * len(names) : 2 * len(names) + 4]
    keys, values, weight, lines, sems = refs[2 * len(names) + 4 :]
    rows = q_ref.shape[0]
    width = KEY_VALUE_HEADS * HEAD_SIZE
    extra = lines.shape[1]
    window = keys.shape[1]
    depth = weight.shape[0] // devices
    own = own_ref[0]
    own_doc = doc_ref[own]

    def copies(i, slot):
        start = pl.multiple_of(slot * rows, rows)
        made = []
        for g in range(KEY_VALUE_HEADS):
            for part, buffer in enumerate((keys, values)):
                column = part * width + g * HEAD_SIZE
                made.append(
                    pltpu.make_async_copy(
                        head_refs[i].at[pl.ds(0, rows), pl.ds(column, HEAD_SIZE)],
                        buffer.at[g, pl.ds(start, rows), pl.ds(0, HEAD_SIZE)],
                        sems.at[i, len(made)],
                    )
                )
        return made

    def line_copy(i):
        return pltpu.make_async_copy(
            head_refs[i].at[pl.ds(rows, extra), :], lines.at[i], sems.at[i, 4]
        )

    def weight_copies(i):
        start = pl.multiple_of(block_of(own, names[i], devices) * depth, depth)
        behind = tail_refs[i].shape[0] - weight.shape[1] // (2 * width) * depth
        return [
            pltpu.make_async_copy(
                tail_refs[i].at[pl.ds(behind + n * depth, depth), :],
                weight.at[pl.ds(start, depth), pl.ds(2 * width * n, 2 * width)],
                sems.at[i, 5 + n],
            )
            for n in range(weight.shape[1] // (2 * width))
        ]

    for c in copies(0, 0):
        c.start()
    slots, seen = [jnp.int32(0)], [True]
    filled = jnp.int32(1)
    for i in range(1, len(names)):
        block = block_of(own, names[i], devices)
        shown = (block < own) & ((block == 0) | (doc_ref[block] == own_doc))
        slots.append(filled)
        seen.append(shown)

        @pl.when(shown)
        def _(i=i, slot=filled):
            for c in copies(i, slot):
                c.start()

        filled = filled + shown.astype(jnp.int32)
    for i in range(len(names)):
        line_copy(i).start()
    for i in range(len(names)):
        for c in weight_copies(i):
            c.start()

    lane = lax.broadcasted_iota(jnp.int32, (window, HEAD_SIZE), 1)
    row = lax.broadcasted_iota(jnp.int32, (window, HEAD_SIZE), 0)
    one_column = jnp.where((lane == 0) & (row < filled * rows), 1.0, 0.0).astype(BF16)
    for g in range(KEY_VALUE_HEADS):
        values[g, :, HEAD_SIZE:] = one_column
    for c in copies(0, 0):
        c.wait()
    for s in range(1, window // rows):

        @pl.when(s >= filled)
        def _(s=s):
            for g in range(KEY_VALUE_HEADS):
                keys[g, s * rows : (s + 1) * rows, :] = jnp.broadcast_to(
                    keys[g, :1, :].astype(F32), (rows, HEAD_SIZE)
                ).astype(BF16)
                values[g, s * rows : (s + 1) * rows, :HEAD_SIZE] = jnp.zeros(
                    (rows, HEAD_SIZE), BF16
                )

    for i in range(1, len(names)):

        @pl.when(seen[i])
        def _(i=i):
            for c in copies(i, slots[i]):
                c.wait()

    query_row = lax.broadcasted_iota(jnp.int32, (rows, rows), 0)
    key_row = lax.broadcasted_iota(jnp.int32, (rows, rows), 1)
    bias = jnp.where(key_row <= query_row, 0.0, -1e30)
    factor = math.log2(math.e) / HEAD_SIZE**0.5
    heads = 4
    for first in range(0, QUERY_HEADS, heads):
        g = first // GROUP
        q = jnp.concatenate(
            [
                q_ref[:, (first + h) * HEAD_SIZE : (first + h + 1) * HEAD_SIZE]
                for h in range(heads)
            ],
            axis=0,
        )
        scores = lax.dot_general(
            q, keys[g], (((1,), (1,)), ((), ())), preferred_element_type=F32
        )
        scores = scores.reshape(heads, rows, window)
        scores = jnp.concatenate([scores[:, :, :rows] + bias[None], scores[:, :, rows:]], axis=2)
        top = jnp.max(scores, axis=-1, keepdims=True)
        probs = jnp.exp2((scores - top) * factor).astype(BF16).reshape(heads * rows, window)
        summed = jnp.dot(probs, values[g], preferred_element_type=F32)
        result = (summed[:, :HEAD_SIZE] / summed[:, HEAD_SIZE : HEAD_SIZE + 1]).astype(BF16)
        for h in range(heads):
            out_ref[:, (first + h) * HEAD_SIZE : (first + h + 1) * HEAD_SIZE] = result[
                h * rows : (h + 1) * rows
            ]

    for i in range(len(names)):
        line_copy(i).wait()
    count = devices * rows // (2 * width)
    in_row = 2 * width // rows
    line = lax.broadcasted_iota(jnp.int32, (extra, 2 * width), 0)
    wanted = (line == own // in_row) | (line == count + own // in_row)
    picked = []
    for i in range(len(names)):
        both = jnp.sum(jnp.where(wanted, lines[i].astype(F32), 0.0), axis=0, keepdims=True)
        picked.append(
            sum(
                jnp.where(own % in_row == n, both[:, n * rows : (n + 1) * rows], 0.0)
                for n in range(in_row)
            )
        )
    picked.append(jnp.zeros((rows - len(names), rows), F32))
    scale_ref[...] = jnp.transpose(jnp.concatenate(picked, axis=0))

    for i in range(len(names)):
        for c in weight_copies(i):
            c.wait()
    hidden = res_ref[...].astype(F32) + jnp.dot(
        out_ref[...], weight[...], preferred_element_type=F32
    )
    hidden_ref[...] = hidden.astype(BF16)
    mean_square = jnp.mean(hidden * hidden, axis=-1, keepdims=True)
    normed_ref[...] = (
        hidden * lax.rsqrt(mean_square + 1e-06) * gain_ref[...].astype(F32)
    ).astype(BF16)


def attend(own, docs, queries, residual, gain, packed, depth, devices):
    rows, model = residual.shape
    window = (min(MOST_BLK, devices) + 1) * rows
    names = piece_names(devices)
    width = KEY_VALUE_HEADS * HEAD_SIZE
    shape = jax.ShapeDtypeStruct(residual.shape, BF16)
    return pl.pallas_call(
        functools.partial(attend_kernel, devices),
        out_shape=(
            jax.ShapeDtypeStruct(queries.shape, BF16),
            jax.ShapeDtypeStruct((rows, rows), F32),
            shape,
            shape,
        ),
        in_specs=[SMEM, SMEM, VMEM, VMEM, VMEM] + [HBM] * (2 * len(names)),
        out_specs=(VMEM,) * 4,
        scratch_shapes=[
            pltpu.VMEM((KEY_VALUE_HEADS, window, HEAD_SIZE), BF16),
            pltpu.VMEM((KEY_VALUE_HEADS, window, 2 * HEAD_SIZE), BF16),
            pltpu.VMEM((depth * devices, model), BF16),
            pltpu.VMEM((len(names), line_rows(devices, rows, width), 2 * width), BF16),
            pltpu.SemaphoreType.DMA((len(names), 5 + model // (2 * width))),
        ],
        compiler_params=PARAMS,
        cost_estimate=pl.CostEstimate(
            flops=4 * QUERY_HEADS * rows * window * HEAD_SIZE + 2 * rows * depth * devices * model,
            bytes_accessed=8 * 2**20,
            transcendentals=QUERY_HEADS * rows * window,
        ),
        name="attend",
    )(
        own,
        docs,
        queries,
        residual,
        gain.reshape(1, -1),
        *[packed[source_of(name, False, devices)] for name in names],
        *[packed[source_of(name, True, devices)] for name in names],
    )


def expert_kernel(parts, scale_ref, gate_ref, up_ref, down_ref, *refs):
    x_refs, out_refs = refs[: len(parts)], refs[len(parts) :]
    x = jnp.concatenate([r[...] for r in x_refs], axis=0)
    gate_part = jnp.dot(x, gate_ref[...], preferred_element_type=F32)
    up_part = jnp.dot(x, up_ref[...], preferred_element_type=F32)
    activated = (gate_part / (1.0 + jnp.exp(-gate_part)) * up_part).astype(BF16)
    produced = jnp.dot(activated, down_ref[...], preferred_element_type=F32)
    half = produced.shape[0] // 2
    at = 0
    for column, start, count in parts:
        part = produced[at : at + count] * scale_ref[start : start + count, column : column + 1]
        out_refs[at // half][at % half : at % half + count, :] = part.astype(BF16)
        at += count


def expert(scale, gate_proj, up_proj, down_proj, parts, pieces):
    rows, width = sum(p.shape[0] for p in pieces), pieces[0].shape[1]
    shape = jax.ShapeDtypeStruct((rows // 2, width), BF16)
    return pl.pallas_call(
        functools.partial(expert_kernel, parts),
        out_shape=(shape, shape),
        in_specs=[VMEM] * (4 + len(pieces)),
        out_specs=(VMEM, VMEM),
        compiler_params=pltpu.CompilerParams(vmem_limit_bytes=32 * 2**20),
        cost_estimate=pl.CostEstimate(
            flops=6 * rows * gate_proj.shape[0] * gate_proj.shape[1],
            bytes_accessed=4 * 2**20,
            transcendentals=rows * gate_proj.shape[1],
        ),
        name="expert",
    )(scale, gate_proj, up_proj, down_proj, *pieces)


def shards(
    queries,
    token_key_heads,
    token_value_heads,
    residual,
    out_weight,
    norm_gain,
    w_gate,
    w_up,
    w_down,
    expert_ids,
    gate_weights,
    doc_of_block,
):
    devices = lax.axis_size("seq")
    own = lax.axis_index("seq").astype(jnp.int32).reshape(1)
    packed = pack(
        token_key_heads, token_value_heads, expert_ids, gate_weights, out_weight, devices
    )
    rows = queries.shape[0]
    cut = rows + line_rows(devices, rows, token_key_heads.shape[1])
    attention, scales, hidden, normed = attend(
        own,
        doc_of_block,
        queries,
        residual,
        norm_gain,
        ring_gather(packed, cut, devices),
        out_weight.shape[0],
        devices,
    )

    half, cut = devices // 4, rows // 2
    tokens = ring_gather(normed, cut, devices)
    names = piece_names(devices)
    kept, sent = {}, {}
    for j, group in enumerate(piece_groups(devices // 2)):
        parts = [(names.index(name), 0, rows) for name in group]
        kept[j], sent[j] = expert(
            scales, w_gate[0], w_up[0], w_down[0], parts, [tokens[name] for name in group]
        )
    near, other = names.index((-half, 0)), names.index((-half, 1))
    parts = [(near, cut, rows - cut), (other, 0, cut), (other, cut, rows - cut), (near, 0, cut)]
    group = [(-half, 0), (-half, 1), (half, 1), (half, 0)]
    kept[half], sent[half] = expert(
        scales, w_gate[0], w_up[0], w_down[0], parts, [tokens[name] for name in group]
    )
    mix = ring_scatter_sum(kept, sent, cut, devices)
    return (attention, hidden, mix)


def solution(mesh):
    in_specs = (
        P(("pack", "seq"), None),
        P(("pack", "seq"), None),
        P(("pack", "seq"), None),
        P(("pack", "seq"), None),
        P("seq", None),
        P(),
        P("seq", None, None),
        P("seq", None, None),
        P("seq", None, None),
        P(("pack", "seq"), None),
        P(("pack", "seq"), None),
        P("pack"),
    )
    out_specs = (P(("pack", "seq"), None), P(("pack", "seq"), None), P(("pack", "seq"), None))
    return jax.shard_map(shards, mesh=mesh, in_specs=in_specs, out_specs=out_specs, check_vma=False)
```

```python
import functools
import math

import jax
import jax.numpy as jnp
from jax import lax
from jax.experimental import pallas as pl
from jax.experimental.pallas import tpu as pltpu
from jax.sharding import PartitionSpec as P

QUERY_HEADS = 16
KEY_VALUE_HEADS = 2
HEAD_SIZE = 128
MOST_BLK = 8
GROUP = QUERY_HEADS // KEY_VALUE_HEADS
F32 = jnp.float32
BF16 = jnp.bfloat16
VMEM_LIMIT = 60 * 1024 * 1024
VMEM = pl.BlockSpec(memory_space=pltpu.VMEM)
SMEM = pl.BlockSpec(memory_space=pltpu.SMEM)
HBM = pl.BlockSpec(memory_space=pl.ANY)
PARAMS = pltpu.CompilerParams(vmem_limit_bytes=VMEM_LIMIT)


def ring_steps(chips):
    order = [2 * i for i in range(chips // 2)] + [2 * i + 1 for i in reversed(range(chips // 2))]
    steps, across = [], []
    for i in range(chips):
        ahead, behind = 2 * order[(i + 1) % chips], 2 * order[i - 1] + 1
        steps += [(2 * order[i], ahead), (2 * order[i] + 1, behind)]
        across += [(2 * order[i] + 1, ahead), (2 * order[i], behind)]
    return steps, across


def swap_steps(devices):
    return [(i, i ^ 1) for i in range(devices)]


def piece_groups(chips):
    groups = [[(0, 0), (0, 1)]]
    for j in range(1, chips // 2):
        groups.append([(-j, 0), (-j, 1), (j, 1), (j, 0)])
    return groups


def piece_names(devices):
    names = [name for group in piece_groups(devices // 2) for name in group]
    return names + [(-(devices // 4), 0), (-(devices // 4), 1)]


def source_of(name, tail, devices):
    half = devices // 4
    if name == (-half, 0):
        return name if tail else (half, 0)
    if name == (-half, 1):
        return (half, 1) if tail else name
    return name


def block_of(own, name, devices):
    chips = devices // 2
    chip, core = own // 2, own % 2
    place = jnp.where(chip % 2 == 0, chip // 2, chips - 1 - chip // 2)
    place = (place + jnp.where(core == 0, name[0], -name[0]) + chips) % chips
    chip = jnp.where(place < chips // 2, 2 * place, 2 * (chips - 1 - place) + 1)
    return 2 * chip + (core if name[1] == 0 else 1 - core)


def ring_gather(piece, cut, devices, aside=None):
    half = devices // 4
    (ring, across), swap = ring_steps(devices // 2), swap_steps(devices)
    pieces = {(0, 0): piece}
    first = second = piece
    for j in range(1, half + 1):
        if j == half and aside is not None:
            first, aside = lax.optimization_barrier((first, aside))
        first = lax.ppermute(first if j < half else first[cut:], "seq", ring)
        second = lax.ppermute(
            second if j < half else second[:cut], "seq", across if j == 1 else ring
        )
        pieces[-j, 0], pieces[-j, 1] = first, second
    pieces[0, 1] = lax.ppermute(piece, "seq", swap)
    for j in range(1, half + 1):
        pieces[j, 1] = lax.ppermute(pieces[-j, 0], "seq", swap)
        pieces[j, 0] = lax.ppermute(pieces[-j, 1], "seq", swap)
    return pieces, aside


def added(*terms):
    return functools.reduce(lambda a, b: a + b, [t.astype(F32) for t in terms])


def ring_scatter_sum(kept, sent, cut, devices):
    half = devices // 4
    ring, across = ring_steps(devices // 2)
    ring, across = [(b, a) for a, b in ring], [(b, a) for a, b in across]
    swap = swap_steps(devices)
    got = {j: lax.ppermute(sent[j], "seq", swap) for j in range(half, -1, -1)}
    rows = kept[0].shape[0]
    first, second = [], []
    for j in range(half, 0, -1):
        if j == half - 1:
            first = [jnp.pad(first[0], ((cut, 0), (0, 0)))]
            second = [jnp.pad(second[0], ((0, rows - cut), (0, 0)))]
        at = rows - cut if j == half else rows
        total = added(kept[j][:at], got[j][:at], *first).astype(BF16)
        _, received = lax.optimization_barrier((total, [got[j][at:], *second]))
        others = added(kept[j][at:], *received).astype(BF16)
        first = [lax.ppermute(total, "seq", ring)]
        second = [lax.ppermute(others, "seq", across if j == 1 else ring)]
    mix = lax.optimization_barrier(added(kept[0], got[0], *first))
    return added(mix, *second).astype(BF16)


def pack_kernel(devices, key_ref, value_ref, id_ref, weight_ref, out_weight_ref, out_ref):
    rows, width = key_ref.shape
    out_ref[:rows, :width] = key_ref[...]
    out_ref[:rows, width:] = value_ref[...]
    ids, weights = id_ref[...], weight_ref[...]
    by_expert = [
        jnp.sum(jnp.where(ids == e, weights, 0.0), axis=0, keepdims=True) for e in range(devices)
    ]
    in_row = 2 * width // rows
    lines = []
    for first in range(0, devices, in_row):
        lines.append(jnp.concatenate(by_expert[first : first + in_row], axis=1))
    high = [line.astype(BF16).astype(F32) for line in lines]
    low = [line - h for line, h in zip(lines, high)]
    extra = line_rows(devices, rows, width)
    if extra > 2 * len(lines):
        low.append(jnp.zeros((extra - 2 * len(lines), 2 * width), F32))
    out_ref[rows : rows + extra, :] = jnp.concatenate(high + low, axis=0).astype(BF16)
    depth = out_weight_ref.shape[0]
    for n in range(out_weight_ref.shape[1] // (2 * width)):
        start = rows + extra + n * depth
        out_ref[start : start + depth, :] = out_weight_ref[:, 2 * width * n : 2 * width * (n + 1)]


def line_rows(devices, rows, width):
    lines = 2 * (devices * rows // (2 * width))
    return -(-lines // 16) * 16


def pack(keys, values, ids, weights, out_weight, devices):
    rows, width = keys.shape
    total = rows + line_rows(devices, rows, width)
    total += out_weight.shape[0] * out_weight.shape[1] // (2 * width)
    return pl.pallas_call(
        functools.partial(pack_kernel, devices),
        out_shape=jax.ShapeDtypeStruct((total, 2 * width), BF16),
        in_specs=[VMEM] * 5,
        out_specs=VMEM,
        compiler_params=PARAMS,
        cost_estimate=pl.CostEstimate(flops=10**6, bytes_accessed=2**20, transcendentals=0),
        name="pack",
    )(keys, values, jnp.transpose(ids), jnp.transpose(weights), out_weight)


def attend_kernel(devices, own_ref, doc_ref, q_ref, res_ref, gain_ref, *refs):
    names = piece_names(devices)
    head_refs, tail_refs = refs[: len(names)], refs[len(names) : 2 * len(names)]
    out_ref, hidden_ref, normed_ref, both, weight, sems = refs[2 * len(names) :]
    rows, model = res_ref.shape
    width = KEY_VALUE_HEADS * HEAD_SIZE
    window = both.shape[0]
    parts = model // (2 * width)
    depth = weight.shape[1] // parts
    own = own_ref[0]
    own_doc = doc_ref[own]

    def kv_copy(i, slot):
        start = pl.multiple_of(slot * rows, rows)
        return pltpu.make_async_copy(
            head_refs[i].at[pl.ds(0, rows), :], both.at[pl.ds(start, rows), :], sems.at[i, 0]
        )

    def weight_copy(i):
        behind = tail_refs[i].shape[0] - parts * depth
        return pltpu.make_async_copy(
            tail_refs[i].at[pl.ds(behind, parts * depth), :],
            weight.at[block_of(own, names[i], devices)],
            sems.at[i, 1],
        )

    kv_copy(0, 0).start()
    slots, seen = [jnp.int32(0)], [True]
    filled = jnp.int32(1)
    for i in range(1, len(names)):
        block = block_of(own, names[i], devices)
        shown = (block < own) & ((block == 0) | (doc_ref[block] == own_doc))
        slots.append(filled)
        seen.append(shown)

        @pl.when(shown)
        def _(i=i, slot=filled):
            kv_copy(i, slot).start()

        filled = filled + shown.astype(jnp.int32)
    for i in range(len(names)):
        weight_copy(i).start()

    kv_copy(0, 0).wait()
    for s in range(1, window // rows):

        @pl.when(s >= filled)
        def _(s=s):
            here = slice(s * rows, (s + 1) * rows)
            both[here, :width] = jnp.broadcast_to(
                both[:1, :width].astype(F32), (rows, width)
            ).astype(BF16)
            both[here, width:] = jnp.zeros((rows, width), BF16)

    for i in range(1, len(names)):

        @pl.when(seen[i])
        def _(i=i):
            kv_copy(i, slots[i]).wait()

    query_row = lax.broadcasted_iota(jnp.int32, (rows, rows), 0)
    key_row = lax.broadcasted_iota(jnp.int32, (rows, rows), 1)
    bias = jnp.where(key_row <= query_row, 0.0, -1e30)
    lane = lax.broadcasted_iota(jnp.int32, (window, HEAD_SIZE), 1)
    row = lax.broadcasted_iota(jnp.int32, (window, HEAD_SIZE), 0)
    one_column = jnp.where((lane == 0) & (row < filled * rows), 1.0, 0.0).astype(BF16)
    factor = math.log2(math.e) / HEAD_SIZE**0.5
    for g in range(KEY_VALUE_HEADS):
        first = g * GROUP
        q = jnp.concatenate(
            [
                q_ref[:, (first + h) * HEAD_SIZE : (first + h + 1) * HEAD_SIZE]
                for h in range(GROUP)
            ],
            axis=0,
        )
        keys = both[:, g * HEAD_SIZE : (g + 1) * HEAD_SIZE]
        values = jnp.concatenate(
            [both[:, width + g * HEAD_SIZE : width + (g + 1) * HEAD_SIZE], one_column], axis=1
        )
        scores = lax.dot_general(q, keys, (((1,), (1,)), ((), ())), preferred_element_type=F32)
        near = (scores[:, :rows].reshape(GROUP, rows, rows) + bias[None]).reshape(-1, rows)
        rest = scores[:, rows:]
        top = jnp.maximum(
            jnp.max(near, axis=-1, keepdims=True), jnp.max(rest, axis=-1, keepdims=True)
        )
        summed = jnp.dot(
            jnp.exp2((near - top) * factor).astype(BF16),
            values[:rows],
            preferred_element_type=F32,
        ) + jnp.dot(
            jnp.exp2((rest - top) * factor).astype(BF16),
            values[rows:],
            preferred_element_type=F32,
        )
        result = (summed[:, :HEAD_SIZE] / summed[:, HEAD_SIZE : HEAD_SIZE + 1]).astype(BF16)
        for h in range(GROUP):
            out_ref[:, (first + h) * HEAD_SIZE : (first + h + 1) * HEAD_SIZE] = result[
                h * rows : (h + 1) * rows
            ]

    for i in range(len(names)):
        weight_copy(i).wait()
    total = []
    for n in range(parts):
        here = res_ref[:, 2 * width * n : 2 * width * (n + 1)].astype(F32)
        for chip in range(devices // 2):
            pair = jnp.concatenate(
                [weight[2 * chip + k, n * depth : (n + 1) * depth, :] for k in range(2)], axis=0
            )
            here += jnp.dot(
                out_ref[:, 2 * depth * chip : 2 * depth * (chip + 1)],
                pair,
                preferred_element_type=F32,
            )
        total.append(here)
    hidden = jnp.concatenate(total, axis=1)
    hidden_ref[...] = hidden.astype(BF16)
    mean_square = jnp.mean(hidden * hidden, axis=-1, keepdims=True)
    normed_ref[...] = (
        hidden * lax.rsqrt(mean_square + 1e-06) * gain_ref[...].astype(F32)
    ).astype(BF16)


def attend(own, docs, queries, residual, gain, packed, depth, devices):
    rows, model = residual.shape
    window = (min(MOST_BLK, devices) + 1) * rows
    names = piece_names(devices)
    width = KEY_VALUE_HEADS * HEAD_SIZE
    parts = model // (2 * width)
    shape = jax.ShapeDtypeStruct(residual.shape, BF16)
    return pl.pallas_call(
        functools.partial(attend_kernel, devices),
        out_shape=(jax.ShapeDtypeStruct(queries.shape, BF16), shape, shape),
        in_specs=[SMEM, SMEM, VMEM, VMEM, VMEM] + [HBM] * (2 * len(names)),
        out_specs=(VMEM,) * 3,
        scratch_shapes=[
            pltpu.VMEM((window, 2 * width), BF16),
            pltpu.VMEM((devices, parts * depth, 2 * width), BF16),
            pltpu.SemaphoreType.DMA((len(names), 2)),
        ],
        compiler_params=PARAMS,
        cost_estimate=pl.CostEstimate(
            flops=4 * QUERY_HEADS * rows * window * HEAD_SIZE + 2 * rows * depth * devices * model,
            bytes_accessed=8 * 2**20,
            transcendentals=QUERY_HEADS * rows * window,
        ),
        name="attend",
    )(
        own,
        docs,
        queries,
        residual,
        gain.reshape(1, -1),
        *[packed[source_of(name, False, devices)] for name in names],
        *[packed[source_of(name, True, devices)] for name in names],
    )


def scales_kernel(devices, rows, width, own_ref, *refs):
    head_refs, (scale_ref, lines, sems) = refs[:-3], refs[-3:]
    own = own_ref[0]
    copies = [
        pltpu.make_async_copy(ref.at[pl.ds(rows, lines.shape[1]), :], lines.at[i], sems.at[i])
        for i, ref in enumerate(head_refs)
    ]
    for c in copies:
        c.start()
    count = devices * rows // (2 * width)
    in_row = 2 * width // rows
    line = lax.broadcasted_iota(jnp.int32, (lines.shape[1], 2 * width), 0)
    wanted = (line == own // in_row) | (line == count + own // in_row)
    picked = []
    for i, c in enumerate(copies):
        c.wait()
        both = jnp.sum(jnp.where(wanted, lines[i].astype(F32), 0.0), axis=0, keepdims=True)
        picked.append(
            sum(
                jnp.where(own % in_row == n, both[:, n * rows : (n + 1) * rows], 0.0)
                for n in range(in_row)
            )
        )
    picked.append(jnp.zeros((rows - len(copies), rows), F32))
    scale_ref[...] = jnp.transpose(jnp.concatenate(picked, axis=0))


def expert_scales(own, packed, rows, devices):
    names = piece_names(devices)
    width = KEY_VALUE_HEADS * HEAD_SIZE
    return pl.pallas_call(
        functools.partial(scales_kernel, devices, rows, width),
        out_shape=jax.ShapeDtypeStruct((rows, rows), F32),
        in_specs=[SMEM] + [HBM] * len(names),
        out_specs=VMEM,
        scratch_shapes=[
            pltpu.VMEM((len(names), line_rows(devices, rows, width), 2 * width), BF16),
            pltpu.SemaphoreType.DMA((len(names),)),
        ],
        compiler_params=PARAMS,
        cost_estimate=pl.CostEstimate(flops=10**6, bytes_accessed=2**19, transcendentals=0),
        name="expert_scales",
    )(own, *[packed[source_of(name, False, devices)] for name in names])


def expert_kernel(parts, scale_ref, gate_ref, up_ref, down_ref, *refs):
    x_refs, out_refs = refs[: len(parts)], refs[len(parts) :]
    x = jnp.concatenate([r[...] for r in x_refs], axis=0)
    gate_part = jnp.dot(x, gate_ref[...], preferred_element_type=F32)
    up_part = jnp.dot(x, up_ref[...], preferred_element_type=F32)
    activated = (gate_part / (1.0 + jnp.exp(-gate_part)) * up_part).astype(BF16)
    produced = jnp.dot(activated, down_ref[...], preferred_element_type=F32)
    half = produced.shape[0] // 2
    at = 0
    for column, start, count in parts:
        part = produced[at : at + count] * scale_ref[start : start + count, column : column + 1]
        out_refs[at // half][at % half : at % half + count, :] = part.astype(BF16)
        at += count


def expert(scale, gate_proj, up_proj, down_proj, parts, pieces):
    rows, width = sum(p.shape[0] for p in pieces), pieces[0].shape[1]
    shape = jax.ShapeDtypeStruct((rows // 2, width), BF16)
    return pl.pallas_call(
        functools.partial(expert_kernel, parts),
        out_shape=(shape, shape),
        in_specs=[VMEM] * (4 + len(pieces)),
        out_specs=(VMEM, VMEM),
        compiler_params=pltpu.CompilerParams(vmem_limit_bytes=32 * 2**20),
        cost_estimate=pl.CostEstimate(
            flops=6 * rows * gate_proj.shape[0] * gate_proj.shape[1],
            bytes_accessed=4 * 2**20,
            transcendentals=rows * gate_proj.shape[1],
        ),
        name="expert",
    )(scale, gate_proj, up_proj, down_proj, *pieces)


def shards(
    queries,
    token_key_heads,
    token_value_heads,
    residual,
    out_weight,
    norm_gain,
    w_gate,
    w_up,
    w_down,
    expert_ids,
    gate_weights,
    doc_of_block,
):
    devices = lax.axis_size("seq")
    own = lax.axis_index("seq").astype(jnp.int32).reshape(1)
    packed = pack(
        token_key_heads, token_value_heads, expert_ids, gate_weights, out_weight, devices
    )
    rows = queries.shape[0]
    cut = rows + line_rows(devices, rows, token_key_heads.shape[1])
    inputs, _ = ring_gather(packed, cut, devices)
    attention, hidden, normed = attend(
        own, doc_of_block, queries, residual, norm_gain, inputs, out_weight.shape[0], devices
    )
    scales = expert_scales(own, inputs, rows, devices)

    half, cut = devices // 4, rows // 2
    tokens, scales = ring_gather(normed, cut, devices, scales)
    names = piece_names(devices)
    kept, sent = {}, {}
    for j, group in enumerate(piece_groups(devices // 2)):
        parts = [(names.index(name), 0, rows) for name in group]
        kept[j], sent[j] = expert(
            scales, w_gate[0], w_up[0], w_down[0], parts, [tokens[name] for name in group]
        )
    near, other = names.index((-half, 0)), names.index((-half, 1))
    parts = [(near, cut, rows - cut), (other, 0, cut), (other, cut, rows - cut), (near, 0, cut)]
    group = [(-half, 0), (-half, 1), (half, 1), (half, 0)]
    kept[half], sent[half] = expert(
        scales, w_gate[0], w_up[0], w_down[0], parts, [tokens[name] for name in group]
    )
    mix = ring_scatter_sum(kept, sent, cut, devices)
    return (attention, hidden, mix)


def solution(mesh):
    in_specs = (
        P(("pack", "seq"), None),
        P(("pack", "seq"), None),
        P(("pack", "seq"), None),
        P(("pack", "seq"), None),
        P("seq", None),
        P(),
        P("seq", None, None),
        P("seq", None, None),
        P("seq", None, None),
        P(("pack", "seq"), None),
        P(("pack", "seq"), None),
        P("pack"),
    )
    out_specs = (P(("pack", "seq"), None), P(("pack", "seq"), None), P(("pack", "seq"), None))
    return jax.shard_map(shards, mesh=mesh, in_specs=in_specs, out_specs=out_specs, check_vma=False)
```

```python
import functools
import math

import jax
import jax.numpy as jnp
from jax import lax
from jax.experimental import pallas as pl
from jax.experimental.pallas import tpu as pltpu
from jax.sharding import PartitionSpec as P

QUERY_HEADS = 16
KEY_VALUE_HEADS = 2
HEAD_SIZE = 128
MOST_BLK = 8
GROUP = QUERY_HEADS // KEY_VALUE_HEADS
F32 = jnp.float32
BF16 = jnp.bfloat16
VMEM_LIMIT = 60 * 1024 * 1024
VMEM = pl.BlockSpec(memory_space=pltpu.VMEM)
SMEM = pl.BlockSpec(memory_space=pltpu.SMEM)
HBM = pl.BlockSpec(memory_space=pl.ANY)
PARAMS = pltpu.CompilerParams(vmem_limit_bytes=VMEM_LIMIT)


def ring_steps(chips):
    order = [2 * i for i in range(chips // 2)] + [2 * i + 1 for i in reversed(range(chips // 2))]
    steps, across = [], []
    for i in range(chips):
        ahead, behind = 2 * order[(i + 1) % chips], 2 * order[i - 1] + 1
        steps += [(2 * order[i], ahead), (2 * order[i] + 1, behind)]
        across += [(2 * order[i] + 1, ahead), (2 * order[i], behind)]
    return steps, across


def swap_steps(devices):
    return [(i, i ^ 1) for i in range(devices)]


def piece_groups(chips):
    groups = [[(0, 0), (0, 1)]]
    for j in range(1, chips // 2):
        groups.append([(-j, 0), (-j, 1), (j, 1), (j, 0)])
    return groups


def piece_names(devices):
    names = [name for group in piece_groups(devices // 2) for name in group]
    return names + [(-(devices // 4), 0), (-(devices // 4), 1)]


def block_of(own, name, devices):
    chips = devices // 2
    chip, core = own // 2, own % 2
    place = jnp.where(chip % 2 == 0, chip // 2, chips - 1 - chip // 2)
    place = (place + jnp.where(core == 0, name[0], -name[0]) + chips) % chips
    chip = jnp.where(place < chips // 2, 2 * place, 2 * (chips - 1 - place) + 1)
    return 2 * chip + (core if name[1] == 0 else 1 - core)


def ring_gather(piece, cut, devices, aside=None, before=None):
    half = devices // 4
    (ring, across), swap = ring_steps(devices // 2), swap_steps(devices)
    pieces = {(0, 0): piece}
    first = second = piece
    for j in range(1, half + 1):
        if j == half and aside is not None:
            first, aside = lax.optimization_barrier((first, aside))
        if before is not None:
            first, second = before(j, first, second)
        first = lax.ppermute(first if j < half else first[cut:], "seq", ring)
        second = lax.ppermute(
            second if j < half else second[:cut], "seq", across if j == 1 else ring
        )
        pieces[-j, 0], pieces[-j, 1] = first, second
    pieces[0, 1] = lax.ppermute(piece, "seq", swap)
    for j in range(1, half + 1):
        pieces[j, 1] = lax.ppermute(pieces[-j, 0], "seq", swap)
        pieces[j, 0] = lax.ppermute(pieces[-j, 1], "seq", swap)
    return pieces, aside


def gather_keys(piece, devices):
    half = devices // 4
    (ring, across), swap = ring_steps(devices // 2), swap_steps(devices)
    pieces = {(0, 0): piece}
    first = second = piece
    for j in range(1, half + 1):
        first = lax.ppermute(first, "seq", ring)
        pieces[-j, 0] = first
        if j < half:
            second = lax.ppermute(second, "seq", across if j == 1 else ring)
            pieces[-j, 1] = second
    pieces[0, 1] = lax.ppermute(piece, "seq", swap)
    for j in range(1, half + 1):
        pieces[-j if j == half else j, 1] = lax.ppermute(pieces[-j, 0], "seq", swap)
        if j < half:
            pieces[j, 0] = lax.ppermute(pieces[-j, 1], "seq", swap)
    return pieces


def added(*terms):
    return functools.reduce(lambda a, b: a + b, [t.astype(F32) for t in terms])


def ring_scatter_sum(kept, sent, cut, devices):
    half = devices // 4
    ring, across = ring_steps(devices // 2)
    ring, across = [(b, a) for a, b in ring], [(b, a) for a, b in across]
    swap = swap_steps(devices)
    got = {j: lax.ppermute(sent[j], "seq", swap) for j in range(half, -1, -1)}
    rows = kept[0].shape[0]
    first, second = [], []
    for j in range(half, 0, -1):
        if j == half - 1:
            first = [jnp.pad(first[0], ((cut, 0), (0, 0)))]
            second = [jnp.pad(second[0], ((0, rows - cut), (0, 0)))]
        at = rows - cut if j == half else rows
        total = added(kept[j][:at], got[j][:at], *first).astype(BF16)
        _, received = lax.optimization_barrier((total, [got[j][at:], *second]))
        others = added(kept[j][at:], *received).astype(BF16)
        first = [lax.ppermute(total, "seq", ring)]
        second = [lax.ppermute(others, "seq", across if j == 1 else ring)]
    mix = lax.optimization_barrier(added(kept[0], got[0], *first))
    return added(mix, *second).astype(BF16)


def pack_kernel(devices, key_ref, value_ref, id_ref, weight_ref, out_ref):
    rows, width = key_ref.shape
    out_ref[:rows, :width] = key_ref[...]
    out_ref[:rows, width:] = value_ref[...]
    ids, weights = id_ref[...], weight_ref[...]
    by_expert = [
        jnp.sum(jnp.where(ids == e, weights, 0.0), axis=0, keepdims=True) for e in range(devices)
    ]
    in_row = 2 * width // rows
    lines = []
    for first in range(0, devices, in_row):
        lines.append(jnp.concatenate(by_expert[first : first + in_row], axis=1))
    high = [line.astype(BF16).astype(F32) for line in lines]
    low = [line - h for line, h in zip(lines, high)]
    extra = line_rows(devices, rows, width)
    if extra > 2 * len(lines):
        low.append(jnp.zeros((extra - 2 * len(lines), 2 * width), F32))
    out_ref[rows : rows + extra, :] = jnp.concatenate(high + low, axis=0).astype(BF16)


def line_rows(devices, rows, width):
    lines = 2 * (devices * rows // (2 * width))
    return -(-lines // 16) * 16


def pack(keys, values, ids, weights, devices):
    rows, width = keys.shape
    total = rows + line_rows(devices, rows, width)
    return pl.pallas_call(
        functools.partial(pack_kernel, devices),
        out_shape=jax.ShapeDtypeStruct((total, 2 * width), BF16),
        in_specs=[VMEM] * 4,
        out_specs=VMEM,
        compiler_params=PARAMS,
        cost_estimate=pl.CostEstimate(flops=10**6, bytes_accessed=2**20, transcendentals=0),
        name="pack",
    )(keys, values, jnp.transpose(ids), jnp.transpose(weights))


def attend_kernel(devices, own_ref, doc_ref, q_ref, *refs):
    names = piece_names(devices)
    head_refs = refs[: len(names)]
    out_ref, scale_ref, both, lines, sems = refs[len(names) :]
    rows = q_ref.shape[0]
    width = KEY_VALUE_HEADS * HEAD_SIZE
    window = both.shape[0]
    own = own_ref[0]
    own_doc = doc_ref[own]

    def kv_copy(i, slot):
        start = pl.multiple_of(slot * rows, rows)
        return pltpu.make_async_copy(
            head_refs[i].at[pl.ds(0, rows), :], both.at[pl.ds(start, rows), :], sems.at[i, 0]
        )

    def line_copy(i):
        return pltpu.make_async_copy(
            head_refs[i].at[pl.ds(rows, lines.shape[1]), :], lines.at[i], sems.at[i, 1]
        )

    kv_copy(0, 0).start()
    slots, seen = [jnp.int32(0)], [True]
    filled = jnp.int32(1)
    for i in range(1, len(names)):
        block = block_of(own, names[i], devices)
        shown = (block < own) & ((block == 0) | (doc_ref[block] == own_doc))
        slots.append(filled)
        seen.append(shown)

        @pl.when(shown)
        def _(i=i, slot=filled):
            kv_copy(i, slot).start()

        filled = filled + shown.astype(jnp.int32)
    for i in range(len(names)):
        line_copy(i).start()

    kv_copy(0, 0).wait()
    for s in range(1, window // rows):

        @pl.when(s >= filled)
        def _(s=s):
            here = slice(s * rows, (s + 1) * rows)
            both[here, :width] = jnp.broadcast_to(
                both[:1, :width].astype(F32), (rows, width)
            ).astype(BF16)
            both[here, width:] = jnp.zeros((rows, width), BF16)

    for i in range(1, len(names)):

        @pl.when(seen[i])
        def _(i=i):
            kv_copy(i, slots[i]).wait()

    query_row = lax.broadcasted_iota(jnp.int32, (rows, rows), 0)
    key_row = lax.broadcasted_iota(jnp.int32, (rows, rows), 1)
    bias = jnp.where(key_row <= query_row, 0.0, -1e30)
    lane = lax.broadcasted_iota(jnp.int32, (window, HEAD_SIZE), 1)
    row = lax.broadcasted_iota(jnp.int32, (window, HEAD_SIZE), 0)
    one_column = jnp.where((lane == 0) & (row < filled * rows), 1.0, 0.0).astype(BF16)
    factor = math.log2(math.e) / HEAD_SIZE**0.5
    for g in range(KEY_VALUE_HEADS):
        first = g * GROUP
        q = jnp.concatenate(
            [
                q_ref[:, (first + h) * HEAD_SIZE : (first + h + 1) * HEAD_SIZE]
                for h in range(GROUP)
            ],
            axis=0,
        )
        keys = both[:, g * HEAD_SIZE : (g + 1) * HEAD_SIZE]
        values = jnp.concatenate(
            [both[:, width + g * HEAD_SIZE : width + (g + 1) * HEAD_SIZE], one_column], axis=1
        )
        scores = lax.dot_general(q, keys, (((1,), (1,)), ((), ())), preferred_element_type=F32)
        near = (scores[:, :rows].reshape(GROUP, rows, rows) + bias[None]).reshape(-1, rows)
        rest = scores[:, rows:]
        top = jnp.maximum(
            jnp.max(near, axis=-1, keepdims=True), jnp.max(rest, axis=-1, keepdims=True)
        )
        summed = jnp.dot(
            jnp.exp2((near - top) * factor).astype(BF16),
            values[:rows],
            preferred_element_type=F32,
        ) + jnp.dot(
            jnp.exp2((rest - top) * factor).astype(BF16),
            values[rows:],
            preferred_element_type=F32,
        )
        result = (summed[:, :HEAD_SIZE] / summed[:, HEAD_SIZE : HEAD_SIZE + 1]).astype(BF16)
        for h in range(GROUP):
            out_ref[:, (first + h) * HEAD_SIZE : (first + h + 1) * HEAD_SIZE] = result[
                h * rows : (h + 1) * rows
            ]

    count = devices * rows // (2 * width)
    in_row = 2 * width // rows
    line = lax.broadcasted_iota(jnp.int32, (lines.shape[1], 2 * width), 0)
    wanted = (line == own // in_row) | (line == count + own // in_row)
    picked = []
    for i in range(len(names)):
        line_copy(i).wait()
        line = jnp.sum(jnp.where(wanted, lines[i].astype(F32), 0.0), axis=0, keepdims=True)
        picked.append(
            sum(
                jnp.where(own % in_row == n, line[:, n * rows : (n + 1) * rows], 0.0)
                for n in range(in_row)
            )
        )
    picked.append(jnp.zeros((rows - len(names), rows), F32))
    scale_ref[...] = jnp.transpose(jnp.concatenate(picked, axis=0))


def attend(own, docs, queries, heads, devices):
    rows = queries.shape[0]
    window = (min(MOST_BLK, devices) + 1) * rows
    names = piece_names(devices)
    width = KEY_VALUE_HEADS * HEAD_SIZE
    return pl.pallas_call(
        functools.partial(attend_kernel, devices),
        out_shape=(
            jax.ShapeDtypeStruct(queries.shape, BF16),
            jax.ShapeDtypeStruct((rows, rows), F32),
        ),
        in_specs=[SMEM, SMEM, VMEM] + [HBM] * len(names),
        out_specs=(VMEM, VMEM),
        scratch_shapes=[
            pltpu.VMEM((window, 2 * width), BF16),
            pltpu.VMEM((len(names), line_rows(devices, rows, width), 2 * width), BF16),
            pltpu.SemaphoreType.DMA((len(names), 2)),
        ],
        compiler_params=PARAMS,
        cost_estimate=pl.CostEstimate(
            flops=4 * QUERY_HEADS * rows * window * HEAD_SIZE,
            bytes_accessed=8 * 2**20,
            transcendentals=QUERY_HEADS * rows * window,
        ),
        name="attend",
    )(own, docs, queries, *[heads[name] for name in names])


def project_kernel(devices, own_ref, att_ref, res_ref, gain_ref, *refs):
    names = piece_names(devices)
    w_refs, (hidden_ref, normed_ref, weight, sems) = refs[:-4], refs[-4:]
    own = own_ref[0]
    depth = weight.shape[0] // devices
    copies = []
    for i, ref in enumerate(w_refs):
        if i < len(names) - 2:
            name, start = names[i], 0
        else:
            far = i - (len(names) - 2)
            name, start = names[len(names) - 2 + far // 2], far % 2 * (depth - ref.shape[0])
        at = pl.multiple_of(block_of(own, name, devices) * depth + start, 16)
        copies.append(
            pltpu.make_async_copy(ref, weight.at[pl.ds(at, ref.shape[0]), :], sems.at[i])
        )
        copies[-1].start()
    for c in copies:
        c.wait()
    hidden = res_ref[...].astype(F32) + jnp.dot(
        att_ref[...], weight[...], preferred_element_type=F32
    )
    hidden_ref[...] = hidden.astype(BF16)
    mean_square = jnp.mean(hidden * hidden, axis=-1, keepdims=True)
    normed_ref[...] = (
        hidden * lax.rsqrt(mean_square + 1e-06) * gain_ref[...].astype(F32)
    ).astype(BF16)


def project(own, attention, residual, gain, pieces, depth, devices):
    names = piece_names(devices)
    half = devices // 4
    refs = [pieces[name] for name in names[:-2]]
    refs += [pieces[name] for name in ((half, 0), (-half, 0), (-half, 1), (half, 1))]
    shape = jax.ShapeDtypeStruct(residual.shape, BF16)
    return pl.pallas_call(
        functools.partial(project_kernel, devices),
        out_shape=(shape, shape),
        in_specs=[SMEM, VMEM, VMEM, VMEM] + [HBM] * len(refs),
        out_specs=(VMEM, VMEM),
        scratch_shapes=[
            pltpu.VMEM((depth * devices, residual.shape[1]), BF16),
            pltpu.SemaphoreType.DMA((len(refs),)),
        ],
        compiler_params=pltpu.CompilerParams(vmem_limit_bytes=24 * 2**20),
        cost_estimate=pl.CostEstimate(
            flops=2 * residual.shape[0] * depth * devices * residual.shape[1],
            bytes_accessed=6 * 2**20,
            transcendentals=0,
        ),
        name="project",
    )(own, attention, residual, gain.reshape(1, -1), *refs)


def expert_kernel(parts, scale_ref, gate_ref, up_ref, down_ref, *refs):
    x_refs, out_refs = refs[: len(parts)], refs[len(parts) :]
    x = jnp.concatenate([r[...] for r in x_refs], axis=0)
    gate_part = jnp.dot(x, gate_ref[...], preferred_element_type=F32)
    up_part = jnp.dot(x, up_ref[...], preferred_element_type=F32)
    activated = (gate_part / (1.0 + jnp.exp(-gate_part)) * up_part).astype(BF16)
    produced = jnp.dot(activated, down_ref[...], preferred_element_type=F32)
    half = produced.shape[0] // 2
    at = 0
    for column, start, count in parts:
        part = produced[at : at + count] * scale_ref[start : start + count, column : column + 1]
        out_refs[at // half][at % half : at % half + count, :] = part.astype(BF16)
        at += count


def expert(scale, gate_proj, up_proj, down_proj, parts, pieces):
    rows, width = sum(p.shape[0] for p in pieces), pieces[0].shape[1]
    shape = jax.ShapeDtypeStruct((rows // 2, width), BF16)
    return pl.pallas_call(
        functools.partial(expert_kernel, parts),
        out_shape=(shape, shape),
        in_specs=[VMEM] * (4 + len(pieces)),
        out_specs=(VMEM, VMEM),
        compiler_params=pltpu.CompilerParams(vmem_limit_bytes=32 * 2**20),
        cost_estimate=pl.CostEstimate(
            flops=6 * rows * gate_proj.shape[0] * gate_proj.shape[1],
            bytes_accessed=4 * 2**20,
            transcendentals=rows * gate_proj.shape[1],
        ),
        name="expert",
    )(scale, gate_proj, up_proj, down_proj, *pieces)


def shards(
    queries,
    token_key_heads,
    token_value_heads,
    residual,
    out_weight,
    norm_gain,
    w_gate,
    w_up,
    w_down,
    expert_ids,
    gate_weights,
    doc_of_block,
):
    devices = lax.axis_size("seq")
    own = lax.axis_index("seq").astype(jnp.int32).reshape(1)
    rows = queries.shape[0]
    packed = pack(token_key_heads, token_value_heads, expert_ids, gate_weights, devices)
    keys = gather_keys(packed, devices)
    half, depth = devices // 4, out_weight.shape[0]
    made = {}

    def before(j, first, second):
        if j == 1:
            pass
        if j == half - 1:
            first, keys[-half, 0] = lax.optimization_barrier((first, keys[-half, 0]))
        if j == half:
            made["attention"], made["scales"] = attend(own, doc_of_block, queries, keys, devices)
            first, second, made["attention"] = lax.optimization_barrier(
                (first, second, made["attention"])
            )
        return first, second

    weights, _ = ring_gather(out_weight, depth // 2, devices, before=before)
    attention, scales = made["attention"], made["scales"]
    hidden, normed = project(own, attention, residual, norm_gain, weights, depth, devices)

    half, cut = devices // 4, rows // 2
    tokens, _ = ring_gather(normed, cut, devices)
    names = piece_names(devices)
    kept, sent = {}, {}
    for j, group in enumerate(piece_groups(devices // 2)):
        parts = [(names.index(name), 0, rows) for name in group]
        kept[j], sent[j] = expert(
            scales, w_gate[0], w_up[0], w_down[0], parts, [tokens[name] for name in group]
        )
    near, other = names.index((-half, 0)), names.index((-half, 1))
    parts = [(near, cut, rows - cut), (other, 0, cut), (other, cut, rows - cut), (near, 0, cut)]
    group = [(-half, 0), (-half, 1), (half, 1), (half, 0)]
    kept[half], sent[half] = expert(
        scales, w_gate[0], w_up[0], w_down[0], parts, [tokens[name] for name in group]
    )
    mix = ring_scatter_sum(kept, sent, cut, devices)
    return (attention, hidden, mix)


def solution(mesh):
    in_specs = (
        P(("pack", "seq"), None),
        P(("pack", "seq"), None),
        P(("pack", "seq"), None),
        P(("pack", "seq"), None),
        P("seq", None),
        P(),
        P("seq", None, None),
        P("seq", None, None),
        P("seq", None, None),
        P(("pack", "seq"), None),
        P(("pack", "seq"), None),
        P("pack"),
    )
    out_specs = (P(("pack", "seq"), None), P(("pack", "seq"), None), P(("pack", "seq"), None))
    return jax.shard_map(shards, mesh=mesh, in_specs=in_specs, out_specs=out_specs, check_vma=False)
```

```python
import functools
import math

import jax
import jax.numpy as jnp
from jax import lax
from jax.experimental import pallas as pl
from jax.experimental.pallas import tpu as pltpu
from jax.sharding import PartitionSpec as P

QUERY_HEADS = 16
KEY_VALUE_HEADS = 2
HEAD_SIZE = 128
MOST_BLK = 8
GROUP = QUERY_HEADS // KEY_VALUE_HEADS
F32 = jnp.float32
BF16 = jnp.bfloat16
VMEM_LIMIT = 60 * 1024 * 1024
VMEM = pl.BlockSpec(memory_space=pltpu.VMEM)
SMEM = pl.BlockSpec(memory_space=pltpu.SMEM)
HBM = pl.BlockSpec(memory_space=pl.ANY)
PARAMS = pltpu.CompilerParams(vmem_limit_bytes=VMEM_LIMIT)


def ring_steps(chips):
    order = [2 * i for i in range(chips // 2)] + [2 * i + 1 for i in reversed(range(chips // 2))]
    steps, across = [], []
    for i in range(chips):
        ahead, behind = 2 * order[(i + 1) % chips], 2 * order[i - 1] + 1
        steps += [(2 * order[i], ahead), (2 * order[i] + 1, behind)]
        across += [(2 * order[i] + 1, ahead), (2 * order[i], behind)]
    return steps, across


def swap_steps(devices):
    return [(i, i ^ 1) for i in range(devices)]


def piece_groups(chips):
    groups = [[(0, 0), (0, 1)]]
    for j in range(1, chips // 2):
        groups.append([(-j, 0), (-j, 1), (j, 1), (j, 0)])
    return groups


def piece_names(devices):
    names = [name for group in piece_groups(devices // 2) for name in group]
    return names + [(-(devices // 4), 0), (-(devices // 4), 1)]


def block_of(own, name, devices):
    chips = devices // 2
    chip, core = own // 2, own % 2
    place = jnp.where(chip % 2 == 0, chip // 2, chips - 1 - chip // 2)
    place = (place + jnp.where(core == 0, name[0], -name[0]) + chips) % chips
    chip = jnp.where(place < chips // 2, 2 * place, 2 * (chips - 1 - place) + 1)
    return 2 * chip + (core if name[1] == 0 else 1 - core)


def ring_gather(piece, cut, devices, aside=None, before=None):
    half = devices // 4
    (ring, across), swap = ring_steps(devices // 2), swap_steps(devices)
    pieces = {(0, 0): piece}
    first = second = piece
    for j in range(1, half + 1):
        if j == half and aside is not None:
            first, aside = lax.optimization_barrier((first, aside))
        if before is not None:
            first, second = before(j, first, second)
        first = lax.ppermute(first if j < half else first[cut:], "seq", ring)
        second = lax.ppermute(
            second if j < half else second[:cut], "seq", across if j == 1 else ring
        )
        pieces[-j, 0], pieces[-j, 1] = first, second
    pieces[0, 1] = lax.ppermute(piece, "seq", swap)
    for j in range(1, half + 1):
        pieces[j, 1] = lax.ppermute(pieces[-j, 0], "seq", swap)
        pieces[j, 0] = lax.ppermute(pieces[-j, 1], "seq", swap)
    return pieces, aside


def gather_keys(piece, devices):
    half = devices // 4
    (ring, across), swap = ring_steps(devices // 2), swap_steps(devices)
    pieces = {(0, 0): piece}
    first = second = piece
    for j in range(1, half + 1):
        first = lax.ppermute(first, "seq", ring)
        pieces[-j, 0] = first
        if j < half:
            second = lax.ppermute(second, "seq", across if j == 1 else ring)
            pieces[-j, 1] = second
    pieces[0, 1] = lax.ppermute(piece, "seq", swap)
    for j in range(1, half + 1):
        pieces[-j if j == half else j, 1] = lax.ppermute(pieces[-j, 0], "seq", swap)
        if j < half:
            pieces[j, 0] = lax.ppermute(pieces[-j, 1], "seq", swap)
    return pieces


def added(*terms):
    return functools.reduce(lambda a, b: a + b, [t.astype(F32) for t in terms])


def ring_scatter_sum(kept, sent, cut, devices):
    half = devices // 4
    ring, across = ring_steps(devices // 2)
    ring, across = [(b, a) for a, b in ring], [(b, a) for a, b in across]
    swap = swap_steps(devices)
    got = {j: lax.ppermute(sent[j], "seq", swap) for j in range(half, -1, -1)}
    rows = kept[0].shape[0]
    first, second = [], []
    for j in range(half, 0, -1):
        if j == half - 1:
            first = [jnp.pad(first[0], ((cut, 0), (0, 0)))]
            second = [jnp.pad(second[0], ((0, rows - cut), (0, 0)))]
        at = rows - cut if j == half else rows
        total = added(kept[j][:at], got[j][:at], *first).astype(BF16)
        _, received = lax.optimization_barrier((total, [got[j][at:], *second]))
        others = added(kept[j][at:], *received).astype(BF16)
        first = [lax.ppermute(total, "seq", ring)]
        second = [lax.ppermute(others, "seq", across if j == 1 else ring)]
    mix = lax.optimization_barrier(added(kept[0], got[0], *first))
    return added(mix, *second).astype(BF16)


def pack_kernel(devices, key_ref, value_ref, id_ref, weight_ref, out_ref):
    rows, width = key_ref.shape
    out_ref[:rows, :width] = key_ref[...]
    out_ref[:rows, width:] = value_ref[...]
    ids, weights = id_ref[...], weight_ref[...]
    by_expert = [
        jnp.sum(jnp.where(ids == e, weights, 0.0), axis=0, keepdims=True) for e in range(devices)
    ]
    in_row = 2 * width // rows
    lines = []
    for first in range(0, devices, in_row):
        lines.append(jnp.concatenate(by_expert[first : first + in_row], axis=1))
    high = [line.astype(BF16).astype(F32) for line in lines]
    low = [line - h for line, h in zip(lines, high)]
    extra = line_rows(devices, rows, width)
    if extra > 2 * len(lines):
        low.append(jnp.zeros((extra - 2 * len(lines), 2 * width), F32))
    out_ref[rows : rows + extra, :] = jnp.concatenate(high + low, axis=0).astype(BF16)


def line_rows(devices, rows, width):
    lines = 2 * (devices * rows // (2 * width))
    return -(-lines // 16) * 16


def pack(keys, values, ids, weights, devices):
    rows, width = keys.shape
    total = rows + line_rows(devices, rows, width)
    return pl.pallas_call(
        functools.partial(pack_kernel, devices),
        out_shape=jax.ShapeDtypeStruct((total, 2 * width), BF16),
        in_specs=[VMEM] * 4,
        out_specs=VMEM,
        compiler_params=PARAMS,
        cost_estimate=pl.CostEstimate(flops=10**6, bytes_accessed=2**20, transcendentals=0),
        name="pack",
    )(keys, values, jnp.transpose(ids), jnp.transpose(weights))


def attend_kernel(devices, own_ref, doc_ref, q_ref, *refs):
    names = piece_names(devices)
    head_refs = refs[: len(names)]
    out_ref, scale_ref, both, lines, sems = refs[len(names) :]
    rows = q_ref.shape[0]
    width = KEY_VALUE_HEADS * HEAD_SIZE
    window = both.shape[0]
    own = own_ref[0]
    own_doc = doc_ref[own]

    def kv_copy(i, slot):
        start = pl.multiple_of(slot * rows, rows)
        return pltpu.make_async_copy(
            head_refs[i].at[pl.ds(0, rows), :], both.at[pl.ds(start, rows), :], sems.at[i, 0]
        )

    def line_copy(i):
        return pltpu.make_async_copy(
            head_refs[i].at[pl.ds(rows, lines.shape[1]), :], lines.at[i], sems.at[i, 1]
        )

    kv_copy(0, 0).start()
    slots, seen = [jnp.int32(0)], [True]
    filled = jnp.int32(1)
    for i in range(1, len(names)):
        block = block_of(own, names[i], devices)
        shown = (block < own) & ((block == 0) | (doc_ref[block] == own_doc))
        slots.append(filled)
        seen.append(shown)

        @pl.when(shown)
        def _(i=i, slot=filled):
            kv_copy(i, slot).start()

        filled = filled + shown.astype(jnp.int32)
    for i in range(len(names)):
        line_copy(i).start()

    kv_copy(0, 0).wait()
    for s in range(1, window // rows):

        @pl.when(s >= filled)
        def _(s=s):
            here = slice(s * rows, (s + 1) * rows)
            both[here, :width] = jnp.broadcast_to(
                both[:1, :width].astype(F32), (rows, width)
            ).astype(BF16)
            both[here, width:] = jnp.zeros((rows, width), BF16)

    for i in range(1, len(names)):

        @pl.when(seen[i])
        def _(i=i):
            kv_copy(i, slots[i]).wait()

    query_row = lax.broadcasted_iota(jnp.int32, (rows, rows), 0)
    key_row = lax.broadcasted_iota(jnp.int32, (rows, rows), 1)
    bias = jnp.where(key_row <= query_row, 0.0, -1e30)
    lane = lax.broadcasted_iota(jnp.int32, (window, HEAD_SIZE), 1)
    row = lax.broadcasted_iota(jnp.int32, (window, HEAD_SIZE), 0)
    one_column = jnp.where((lane == 0) & (row < filled * rows), 1.0, 0.0).astype(BF16)
    factor = math.log2(math.e) / HEAD_SIZE**0.5
    for g in range(KEY_VALUE_HEADS):
        first = g * GROUP
        q = jnp.concatenate(
            [
                q_ref[:, (first + h) * HEAD_SIZE : (first + h + 1) * HEAD_SIZE]
                for h in range(GROUP)
            ],
            axis=0,
        )
        keys = both[:, g * HEAD_SIZE : (g + 1) * HEAD_SIZE]
        values = jnp.concatenate(
            [both[:, width + g * HEAD_SIZE : width + (g + 1) * HEAD_SIZE], one_column], axis=1
        )
        scores = lax.dot_general(q, keys, (((1,), (1,)), ((), ())), preferred_element_type=F32)
        near = (scores[:, :rows].reshape(GROUP, rows, rows) + bias[None]).reshape(-1, rows)
        rest = scores[:, rows:]
        top = jnp.maximum(
            jnp.max(near, axis=-1, keepdims=True), jnp.max(rest, axis=-1, keepdims=True)
        )
        summed = jnp.dot(
            jnp.exp2((near - top) * factor).astype(BF16),
            values[:rows],
            preferred_element_type=F32,
        ) + jnp.dot(
            jnp.exp2((rest - top) * factor).astype(BF16),
            values[rows:],
            preferred_element_type=F32,
        )
        result = (summed[:, :HEAD_SIZE] / summed[:, HEAD_SIZE : HEAD_SIZE + 1]).astype(BF16)
        for h in range(GROUP):
            out_ref[:, (first + h) * HEAD_SIZE : (first + h + 1) * HEAD_SIZE] = result[
                h * rows : (h + 1) * rows
            ]

    count = devices * rows // (2 * width)
    in_row = 2 * width // rows
    line = lax.broadcasted_iota(jnp.int32, (lines.shape[1], 2 * width), 0)
    wanted = (line == own // in_row) | (line == count + own // in_row)
    picked = []
    for i in range(len(names)):
        line_copy(i).wait()
        line = jnp.sum(jnp.where(wanted, lines[i].astype(F32), 0.0), axis=0, keepdims=True)
        picked.append(
            sum(
                jnp.where(own % in_row == n, line[:, n * rows : (n + 1) * rows], 0.0)
                for n in range(in_row)
            )
        )
    picked.append(jnp.zeros((rows - len(names), rows), F32))
    scale_ref[...] = jnp.transpose(jnp.concatenate(picked, axis=0))


def attend(own, docs, queries, heads, devices):
    rows = queries.shape[0]
    window = (min(MOST_BLK, devices) + 1) * rows
    names = piece_names(devices)
    width = KEY_VALUE_HEADS * HEAD_SIZE
    return pl.pallas_call(
        functools.partial(attend_kernel, devices),
        out_shape=(
            jax.ShapeDtypeStruct(queries.shape, BF16),
            jax.ShapeDtypeStruct((rows, rows), F32),
        ),
        in_specs=[SMEM, SMEM, VMEM] + [HBM] * len(names),
        out_specs=(VMEM, VMEM),
        scratch_shapes=[
            pltpu.VMEM((window, 2 * width), BF16),
            pltpu.VMEM((len(names), line_rows(devices, rows, width), 2 * width), BF16),
            pltpu.SemaphoreType.DMA((len(names), 2)),
        ],
        compiler_params=PARAMS,
        cost_estimate=pl.CostEstimate(
            flops=4 * QUERY_HEADS * rows * window * HEAD_SIZE,
            bytes_accessed=8 * 2**20,
            transcendentals=QUERY_HEADS * rows * window,
        ),
        name="attend",
    )(own, docs, queries, *[heads[name] for name in names])


def project_kernel(devices, own_ref, att_ref, res_ref, gain_ref, *refs):
    names = piece_names(devices)
    w_refs, (hidden_ref, normed_ref, weight, sems) = refs[:-4], refs[-4:]
    own = own_ref[0]
    depth = weight.shape[0] // devices
    copies = []
    for i, ref in enumerate(w_refs):
        if i < len(names) - 2:
            name, start = names[i], 0
        else:
            far = i - (len(names) - 2)
            name, start = names[len(names) - 2 + far // 2], far % 2 * (depth - ref.shape[0])
        at = pl.multiple_of(block_of(own, name, devices) * depth + start, 16)
        copies.append(
            pltpu.make_async_copy(ref, weight.at[pl.ds(at, ref.shape[0]), :], sems.at[i])
        )
        copies[-1].start()
    for c in copies:
        c.wait()
    hidden = res_ref[...].astype(F32) + jnp.dot(
        att_ref[...], weight[...], preferred_element_type=F32
    )
    hidden_ref[...] = hidden.astype(BF16)
    mean_square = jnp.mean(hidden * hidden, axis=-1, keepdims=True)
    normed_ref[...] = (
        hidden * lax.rsqrt(mean_square + 1e-06) * gain_ref[...].astype(F32)
    ).astype(BF16)


def project(own, attention, residual, gain, pieces, depth, devices):
    names = piece_names(devices)
    half = devices // 4
    refs = [pieces[name] for name in names[:-2]]
    refs += [pieces[name] for name in ((half, 0), (-half, 0), (-half, 1), (half, 1))]
    shape = jax.ShapeDtypeStruct(residual.shape, BF16)
    return pl.pallas_call(
        functools.partial(project_kernel, devices),
        out_shape=(shape, shape),
        in_specs=[SMEM, VMEM, VMEM, VMEM] + [HBM] * len(refs),
        out_specs=(VMEM, VMEM),
        scratch_shapes=[
            pltpu.VMEM((depth * devices, residual.shape[1]), BF16),
            pltpu.SemaphoreType.DMA((len(refs),)),
        ],
        compiler_params=pltpu.CompilerParams(vmem_limit_bytes=14 * 2**20),
        cost_estimate=pl.CostEstimate(
            flops=2 * residual.shape[0] * depth * devices * residual.shape[1],
            bytes_accessed=6 * 2**20,
            transcendentals=0,
        ),
        name="project",
    )(own, attention, residual, gain.reshape(1, -1), *refs)


def expert_kernel(parts, scale_ref, gate_ref, up_ref, down_ref, *refs):
    x_refs, out_refs = refs[: len(parts)], refs[len(parts) :]
    x = jnp.concatenate([r[...] for r in x_refs], axis=0)
    gate_part = jnp.dot(x, gate_ref[...], preferred_element_type=F32)
    up_part = jnp.dot(x, up_ref[...], preferred_element_type=F32)
    activated = (gate_part / (1.0 + jnp.exp(-gate_part)) * up_part).astype(BF16)
    produced = jnp.dot(activated, down_ref[...], preferred_element_type=F32)
    half = produced.shape[0] // 2
    at = 0
    for column, start, count in parts:
        part = produced[at : at + count] * scale_ref[start : start + count, column : column + 1]
        out_refs[at // half][at % half : at % half + count, :] = part.astype(BF16)
        at += count


def expert(scale, gate_proj, up_proj, down_proj, parts, pieces):
    rows, width = sum(p.shape[0] for p in pieces), pieces[0].shape[1]
    shape = jax.ShapeDtypeStruct((rows // 2, width), BF16)
    return pl.pallas_call(
        functools.partial(expert_kernel, parts),
        out_shape=(shape, shape),
        in_specs=[VMEM] * (4 + len(pieces)),
        out_specs=(VMEM, VMEM),
        compiler_params=pltpu.CompilerParams(vmem_limit_bytes=32 * 2**20),
        cost_estimate=pl.CostEstimate(
            flops=6 * rows * gate_proj.shape[0] * gate_proj.shape[1],
            bytes_accessed=4 * 2**20,
            transcendentals=rows * gate_proj.shape[1],
        ),
        name="expert",
    )(scale, gate_proj, up_proj, down_proj, *pieces)


def shards(
    queries,
    token_key_heads,
    token_value_heads,
    residual,
    out_weight,
    norm_gain,
    w_gate,
    w_up,
    w_down,
    expert_ids,
    gate_weights,
    doc_of_block,
):
    devices = lax.axis_size("seq")
    own = lax.axis_index("seq").astype(jnp.int32).reshape(1)
    rows = queries.shape[0]
    packed = pack(token_key_heads, token_value_heads, expert_ids, gate_weights, devices)
    keys = gather_keys(packed, devices)
    half, depth = devices // 4, out_weight.shape[0]
    made = {}

    def before(j, first, second):
        if j == 1:
            pass
        if j == half - 1:
            first, keys[-half, 0] = lax.optimization_barrier((first, keys[-half, 0]))
        if j == half:
            made["attention"], made["scales"] = attend(own, doc_of_block, queries, keys, devices)
            first, second, made["attention"] = lax.optimization_barrier(
                (first, second, made["attention"])
            )
        return first, second

    weights, _ = ring_gather(out_weight, depth // 2, devices, before=before)
    attention, scales = made["attention"], made["scales"]
    hidden, normed = project(own, attention, residual, norm_gain, weights, depth, devices)

    half, cut = devices // 4, rows // 8 * 5
    tokens, _ = ring_gather(normed, cut, devices)
    names = piece_names(devices)
    kept, sent = {}, {}
    for j, group in enumerate(piece_groups(devices // 2)):
        parts = [(names.index(name), 0, rows) for name in group]
        kept[j], sent[j] = expert(
            scales, w_gate[0], w_up[0], w_down[0], parts, [tokens[name] for name in group]
        )
    near, other = names.index((-half, 0)), names.index((-half, 1))
    parts = [(near, cut, rows - cut), (other, 0, cut), (other, cut, rows - cut), (near, 0, cut)]
    group = [(-half, 0), (-half, 1), (half, 1), (half, 0)]
    kept[half], sent[half] = expert(
        scales, w_gate[0], w_up[0], w_down[0], parts, [tokens[name] for name in group]
    )
    mix = ring_scatter_sum(kept, sent, cut, devices)
    return (attention, hidden, mix)


def solution(mesh):
    in_specs = (
        P(("pack", "seq"), None),
        P(("pack", "seq"), None),
        P(("pack", "seq"), None),
        P(("pack", "seq"), None),
        P("seq", None),
        P(),
        P("seq", None, None),
        P("seq", None, None),
        P("seq", None, None),
        P(("pack", "seq"), None),
        P(("pack", "seq"), None),
        P("pack"),
    )
    out_specs = (P(("pack", "seq"), None), P(("pack", "seq"), None), P(("pack", "seq"), None))
    return jax.shard_map(shards, mesh=mesh, in_specs=in_specs, out_specs=out_specs, check_vma=False)
```
